256 devices in a mesh: dp: 32 (over x_lo, z, core), tensor: 8 (over y, x_hi).
Axes of the slice: x: 4 (x_hi: 2, x_lo: 2; x = x_hi * 2 + x_lo), y: 4, z: 8, core: 2. Of those that a mesh axis runs over, the one named last changes fastest.
Arguments:
- activations: bfloat16 [64, 512, 9216], P('dp', 'tensor'), may hold values from -6 to 6
- w_query: bfloat16 [9216, 4608], P('dp', 'tensor'), may hold values from -0.0625 to 0.0625
- key_weight_latent: bfloat16 [9216, 768], P('dp', 'tensor'), may hold values from -0.0625 to 0.0625
- query_exponent: int32 [4608], P('tensor'), may hold values from -13 to -11
- key_column_exponent: int32 [768], P('tensor'), may hold values from -13 to -11
- queries: bfloat16 [64, 512, 4608], P('dp', None, 'tensor'), may hold values from -6 to 6
- keys: bfloat16 [64, 512, 768], P('dp', None, 'tensor'), may hold values from -6 to 6
- teacher_attention_logits: bfloat16 [64, 48, 512, 512], P('dp', 'tensor'), may hold values from -8 to 8
- document_length: int32 [64, 4], P('dp'), may hold values from 1 to 256, 512 in all within a row
Outputs:
- grad_query: float32 [9216, 4608], P('dp', 'tensor')
- grad_key: float32 [9216, 768], P('dp', 'tensor')
The draws below stay inside these ranges and needn't reach their ends.
Inputs may be any that keep to these rules, and one draw needn't show every extreme that they name: `document_length`: each group's lengths sum to 512.
All inputs are finite; a program needn't handle non-finite values.
Results may differ from the reference program's by a relative error of at most 0.029.
Values may be sent and summed in bfloat16 or wider, within the bound.
No kernel may reach another device: no remote copies, remote signals or barrier semaphores. Data moves between devices by JAX's collectives and lax.ppermute only.
A program may use at most 128 MiB of HBM per device.

```python
import math
import jax
import jax.numpy as jnp
import numpy as np
from jax import lax

MODEL_DIM = 9216
HEAD_DIM = 96
QUERIES_PER_KEY = 6
GROUP_TOKENS = 512
GROUPS_PER_SHARD = 2
DOCS_PER_GROUP = 4
QUANT_EXPONENT = 12
TOKEN_GROUPS = 64
KEY_HEADS = 8
QUERY_HEADS = 48


def plant(result, rng, low, top_value):
    longest = result.shape.index(max(result.shape))
    spots = []
    for shift in (0, 1):
        where = [jax.random.randint(jax.random.fold_in(rng, axis), (), 0, length) for axis, length in enumerate(result.shape)]
        where[longest] = (where[longest] + shift) % result.shape[longest]
        spots.append(tuple(where))
    return result.at[spots[0]].set(low).at[spots[1]].set(top_value)


def raised(drawn, rng, source, target, parts, factor):
    owner, partner = [(jnp.arange(drawn.shape[axis_at]) // (drawn.shape[axis_at] // parts)).reshape([-1 if axis == axis_at else 1 for axis in range(drawn.ndim)]) for axis_at in (source, target)]
    chosen = jax.random.permutation(rng, parts)[partner]
    strong = (owner == chosen) | (owner == (partner + parts // 2) % parts)
    return jnp.where(strong, factor * drawn, drawn)


def steps_of(stream_key, extent, split, low, high):
    loudness, own = 1.0, jax.random.fold_in(stream_key, 6)
    for axis_at, shards_of in split:
        steps = jnp.exp(jax.random.uniform(jax.random.fold_in(own, axis_at), (shards_of,), jnp.float32, low / len(split), high / len(split)))
        loudness = loudness * jnp.repeat(steps, extent[axis_at] // shards_of).reshape([-1 if axis == axis_at else 1 for axis in range(len(extent))])
    return loudness


def split_up(count, total, reach, skew):
    weights = [(1 << 20) // math.isqrt(standing ** skew) + 1 for standing in range(2, count + 1)]
    surplus, given = total - reach - (count - 1), [1] * (count - 1)
    while surplus > 0:
        movable = [i for i in range(count - 1) if given[i] < reach]
        pool, left = sum([weights[i] for i in movable]), surplus
        for i in movable:
            extra = min(reach - given[i], max(1, left * weights[i] // pool), surplus)
            given[i] = given[i] + extra
            surplus = surplus - extra
    return np.array([reach] + given)


def ragged(stream_key, number_of, total, most, skew):
    if number_of == 2:
        one = jax.random.randint(stream_key, (), max(1, total - most), min(most, total - 1) + 1)
        return jnp.stack([one, total - one])
    tallies = jnp.asarray(split_up(number_of, total, most, skew), jnp.int32)
    twos = (number_of - 1) // 2
    giver, receiver = tallies[1:1 + 2 * twos:2], tallies[2:2 + 2 * twos:2]
    margin = jnp.minimum(giver - 1, most - receiver)
    passed = jax.random.randint(jax.random.fold_in(stream_key, 1), (twos,), 0, 1 << 20) % (margin + 1)
    tallies = tallies.at[1:1 + 2 * twos:2].set(giver - passed).at[2:2 + 2 * twos:2].set(receiver + passed)
    return tallies[jax.random.permutation(jax.random.fold_in(stream_key, 2), number_of)]


def bell_draw(rng, shape, spread, bound, cuts=(), kind=jnp.bfloat16):
    array = jax.random.normal(rng, shape, jnp.float32) * spread
    if len(cuts) > 0:
        array = steps_of(rng, shape, cuts, -0.22, 0.18) * array
    return jnp.clip(array, min=-bound, max=bound).astype(kind)


def bell_draw_with(key, extent, width, bound, split, heavy, kind=jnp.bfloat16):
    array = width * jax.random.normal(key, extent, jnp.float32)
    if split:
        array = array * steps_of(key, extent, split, -0.22, 0.18)
    return jnp.clip(raised(array, jax.random.fold_in(key, 3), *heavy), -bound, bound).astype(kind)


def setup_inputs(seed: int = 0) -> dict:
    key_of = jax.random.split(jax.random.key(seed), 10)
    return {
        "activations": bell_draw_with(key_of[0], (TOKEN_GROUPS, GROUP_TOKENS, MODEL_DIM), 1.0, 6.0, ((0, 32), (1, 8)), (0, 2, 32, 2.75)),
        "w_query": bell_draw(key_of[1], (MODEL_DIM, QUERY_HEADS * HEAD_DIM), MODEL_DIM ** -0.5, 0.0625, ((0, 32), (1, 8))),
        "key_weight_latent": bell_draw(key_of[2], (MODEL_DIM, KEY_HEADS * HEAD_DIM), MODEL_DIM ** -0.5, 0.0625, ((0, 32), (1, 8))),
        "query_exponent": plant(jax.random.randint(key_of[3], (QUERY_HEADS * HEAD_DIM,), -QUANT_EXPONENT - 1, 2 - QUANT_EXPONENT), jax.random.fold_in(key_of[3], 1), -QUANT_EXPONENT - 1, (2 - QUANT_EXPONENT) - 1).astype(jnp.int32),
        "key_column_exponent": plant(jax.random.randint(key_of[4], (KEY_HEADS * HEAD_DIM,), -QUANT_EXPONENT - 1, 2 - QUANT_EXPONENT), jax.random.fold_in(key_of[4], 1), -QUANT_EXPONENT - 1, (2 - QUANT_EXPONENT) - 1).astype(jnp.int32),
        "queries": bell_draw(key_of[5], (TOKEN_GROUPS, GROUP_TOKENS, QUERY_HEADS * HEAD_DIM), 1.0, 6.0, ((0, 32), (2, 8))),
        "keys": bell_draw(key_of[6], (TOKEN_GROUPS, GROUP_TOKENS, KEY_HEADS * HEAD_DIM), 1.0, 6.0, ((0, 32), (2, 8))),
        "teacher_attention_logits": bell_draw(key_of[7], (TOKEN_GROUPS, QUERY_HEADS, GROUP_TOKENS, GROUP_TOKENS), 2.0, 8.0, ((0, 32), (1, 8))),
        "document_length": jax.vmap(lambda own: ragged(own, DOCS_PER_GROUP, GROUP_TOKENS, GROUP_TOKENS // 2, 2))(jax.random.split(key_of[8], TOKEN_GROUPS)).reshape((TOKEN_GROUPS, DOCS_PER_GROUP)).astype(jnp.int32),
    }


SOFT_CAP = 30.0
LOSS_SCALE = 64.0

def inside_mask(latent, exponent):
    quant_step = jnp.exp2(exponent.astype(jnp.float32))
    levels = jnp.floor(latent.astype(jnp.float32) / quant_step + 0.5)
    return (jnp.abs(levels) <= 127.0).astype(jnp.float32)

def allowed_pairs(length_row, token_inputs):
    doc_ends = jnp.cumsum(length_row.astype(jnp.int32))
    position = jnp.arange(token_inputs, dtype=jnp.int32)
    segment = lax.optimization_barrier(jnp.sum((position[:, None] >= doc_ends[None, :]).astype(jnp.int32), axis=1))
    return (segment[:, None] == segment[None, :]) & (position[None, :] <= position[:, None])

def softmax_with_mask(logits, attend_mask):
    weights = jnp.where(attend_mask, jnp.exp(logits), 0.0)
    return weights / lax.optimization_barrier(jnp.sum(weights, axis=-1, keepdims=True))

def head_grads(query_token_rows, key_token_rows, teacher_token_rows, length_row):
    token_inputs = query_token_rows.shape[0]
    query_head_split = query_token_rows.astype(jnp.float32).reshape(token_inputs, KEY_HEADS, QUERIES_PER_KEY, HEAD_DIM)
    key_head_split = key_token_rows.astype(jnp.float32).reshape(token_inputs, KEY_HEADS, HEAD_DIM)
    scores = jnp.einsum('tgnd,sgd->gnts', query_head_split, key_head_split) / math.sqrt(HEAD_DIM)
    capped = SOFT_CAP * jnp.tanh(scores / SOFT_CAP)
    attend_mask = allowed_pairs(length_row, token_inputs)
    student = softmax_with_mask(capped, attend_mask)
    teacher_probs = softmax_with_mask(teacher_token_rows.astype(jnp.float32).reshape(KEY_HEADS, QUERIES_PER_KEY, token_inputs, token_inputs), attend_mask)
    slope = 1.0 - (capped / SOFT_CAP) ** 2
    rounded = ((student - teacher_probs) * slope * (LOSS_SCALE / math.sqrt(HEAD_DIM))).astype(jnp.bfloat16)
    logit_gradient = lax.optimization_barrier(rounded).astype(jnp.float32)
    query_grad = jnp.einsum('gnts,sgd->tgnd', logit_gradient, key_head_split).reshape(token_inputs, QUERY_HEADS * HEAD_DIM).astype(jnp.bfloat16)
    key_gradient = jnp.einsum('vkxm,xvka->mva', logit_gradient, query_head_split).reshape(token_inputs, KEY_HEADS * HEAD_DIM).astype(jnp.bfloat16)
    return (query_grad, key_gradient)

def block_terms(activation_block, query_block, key_block, teacher_block, length_block):
    query_list = []
    key_list = []
    for member in range(GROUPS_PER_SHARD):
        query_grad, key_gradient = head_grads(query_block[member], key_block[member], teacher_block[member], length_block[member])
        query_list.append(query_grad)
        key_list.append(key_gradient)
    query_flat = jnp.concatenate(query_list, axis=0)
    key_flat = jnp.concatenate(key_list, axis=0)
    activation_flat = activation_block.reshape(GROUPS_PER_SHARD * GROUP_TOKENS, MODEL_DIM)
    query_term = jnp.dot(activation_flat.T, query_flat, preferred_element_type=jnp.float32).astype(jnp.bfloat16)
    key_term = jnp.dot(activation_flat.T, key_flat, preferred_element_type=jnp.float32).astype(jnp.bfloat16)
    return (query_term, key_term)

def reference(activations, w_query, key_weight_latent, query_exponent, key_column_exponent, queries, keys, teacher_attention_logits, document_length):
    query_inside = inside_mask(w_query, query_exponent[None, :])
    key_inside = inside_mask(key_weight_latent, key_column_exponent[None, :])
    block_list = TOKEN_GROUPS // GROUPS_PER_SHARD

    def advance(carry, inputs):
        query_total, key_total = carry
        query_term, key_term = block_terms(inputs[0], inputs[1], inputs[2], inputs[3], inputs[4])
        query_term, key_term = lax.optimization_barrier((query_term, key_term))
        query_total = query_total + query_term.astype(jnp.float32)
        key_total = key_total + key_term.astype(jnp.float32)
        return ((query_total, key_total), None)
    stacked_blocks = (activations.reshape(block_list, GROUPS_PER_SHARD, GROUP_TOKENS, MODEL_DIM), queries.reshape(block_list, GROUPS_PER_SHARD, GROUP_TOKENS, QUERY_HEADS * HEAD_DIM), keys.reshape(block_list, GROUPS_PER_SHARD, GROUP_TOKENS, KEY_HEADS * HEAD_DIM), teacher_attention_logits.reshape(block_list, GROUPS_PER_SHARD, QUERY_HEADS, GROUP_TOKENS, GROUP_TOKENS), document_length.reshape(block_list, GROUPS_PER_SHARD, DOCS_PER_GROUP))
    initial = (jnp.zeros(w_query.shape, jnp.float32), jnp.zeros(key_weight_latent.shape, jnp.float32))
    (query_total, key_total), unused = lax.scan(advance, initial, stacked_blocks)
    grad_query = query_inside * query_total / LOSS_SCALE
    grad_key = key_inside * key_total / LOSS_SCALE
    return (grad_query, grad_key)
```

```python
import functools
import math

import jax
import jax.numpy as jnp
from jax import lax
from jax.experimental import pallas as pl
from jax.experimental.pallas import tpu as pltpu
from jax.sharding import PartitionSpec as P

SOFT_CAP = 30.0
LOSS_SCALE = 64.0
GROUPS = 2
TOKENS = 512
HEADS = 6
DIM = 96
WIDTH = 672
ROWS = 72
RINGS = 8
BAND = 128
SHARDS = 8
SHARE = 64
NARROW = jnp.bfloat16
MIB = 1024 * 1024
PIECE = 2 * ROWS


def cost(time):
    return pl.CostEstimate(flops=1000, bytes_accessed=int(time * 3.5e6), transcendentals=0)


def spread_tokens(first, second):
    parts = []
    for shard in range(SHARDS):
        parts.append(first[:, shard * SHARE : (shard + 1) * SHARE])
        parts.append(second[:, shard * SHARE : (shard + 1) * SHARE])
    return jnp.concatenate(parts, axis=1).astype(NARROW)


def head_kernel(length_ref, query_ref, key_ref, teacher_ref, *refs):
    out_ref, grad_ref, query_acc, key_acc = refs[-4:]
    head = pl.program_id(0)
    group = pl.program_id(1)

    @pl.when((head == 0) & (group == 0))
    def _():
        grad_ref[...] = jnp.zeros_like(grad_ref)

    ends = [length_ref[group, 0]]
    for document in range(1, length_ref.shape[1]):
        ends.append(ends[-1] + length_ref[group, document])
    query_t = query_ref[0]
    key_t = key_ref[0]
    for first in range(0, TOKENS, BAND):
        low = max(0, first - 2 * BAND)
        high = first + BAND
        token = lax.broadcasted_iota(jnp.int32, (BAND, 1), 0) + first
        start = jnp.zeros_like(token)
        for end in ends:
            start = jnp.where(token >= end, end, start)
        column = lax.broadcasted_iota(jnp.int32, (BAND, high - low), 1) + low
        allowed = (column >= start) & (column <= token)
        dots = lax.dot_general(
            query_t[:, first : first + BAND],
            key_t[:, low:high],
            (((0,), (0,)), ((), ())),
            preferred_element_type=jnp.float32,
        )
        bent = jnp.tanh(dots * (1.0 / (math.sqrt(DIM) * SOFT_CAP)))
        student = jnp.where(allowed, jnp.exp(bent * SOFT_CAP), 0.0)
        logits = teacher_ref[0, 0, first : first + BAND, low:high].astype(jnp.float32)
        teacher = jnp.where(allowed, jnp.exp(logits), 0.0)
        student_scale = 1.0 / jnp.sum(student, axis=1, keepdims=True)
        teacher_scale = 1.0 / jnp.sum(teacher, axis=1, keepdims=True)
        scale = LOSS_SCALE / math.sqrt(DIM)
        slope = scale - scale * (bent * bent)
        grad = (student * student_scale - teacher * teacher_scale) * slope
        grad_ref[first : first + BAND, low:high] = grad.astype(NARROW)
    score_grad = grad_ref[...]
    query_grad = lax.dot_general(
        key_t, score_grad, (((1,), (1,)), ((), ())), preferred_element_type=jnp.float32
    )
    key_grad = lax.dot_general(
        query_t, score_grad, (((1,), (0,)), ((), ())), preferred_element_type=jnp.float32
    )

    @pl.when(head == 0)
    def _():
        key_acc[group] = key_grad

    @pl.when(head != 0)
    def _():
        key_acc[group] = key_acc[group] + key_grad

    @pl.when(group == 0)
    def _():
        query_acc[...] = query_grad

    @pl.when(group == GROUPS - 1)
    def _():
        out_ref[head] = spread_tokens(query_acc[...], query_grad)

    @pl.when((head == HEADS - 1) & (group == GROUPS - 1))
    def _():
        out_ref[HEADS] = spread_tokens(key_acc[0], key_acc[1])


def head_grads(queries, keys, teacher, lengths, after):
    query_t = jnp.swapaxes(queries, 1, 2)
    key_t = jnp.swapaxes(keys, 1, 2)
    shape = (HEADS + 1, DIM, GROUPS * TOKENS)
    out = pl.pallas_call(
        head_kernel,
        out_shape=jax.ShapeDtypeStruct(shape, NARROW),
        grid=(HEADS, GROUPS),
        in_specs=[
            pl.BlockSpec(memory_space=pltpu.SMEM),
            pl.BlockSpec((1, DIM, TOKENS), lambda h, g: (g, h, 0)),
            pl.BlockSpec((1, DIM, TOKENS), lambda h, g: (g, 0, 0)),
            pl.BlockSpec((1, 1, TOKENS, TOKENS), lambda h, g: (g, h, 0, 0)),
        ]
        + [pl.BlockSpec(memory_space=pl.ANY)] * len(after),
        out_specs=pl.BlockSpec(shape, lambda h, g: (0, 0, 0)),
        scratch_shapes=[
            pltpu.VMEM((TOKENS, TOKENS), NARROW),
            pltpu.VMEM((DIM, TOKENS), jnp.float32),
            pltpu.VMEM((GROUPS, DIM, TOKENS), jnp.float32),
        ],
        compiler_params=pltpu.CompilerParams(vmem_limit_bytes=12 * MIB),
        cost_estimate=cost(14),
        name="head_grads",
    )(lengths, query_t, key_t, teacher, *after)
    return out.reshape(WIDTH, GROUPS * TOKENS)


def turn_kernel(place_ref, near_ref, far_ref, *refs):
    turned = refs[4]
    mine = place_ref[0]
    core = place_ref[2]
    lanes = near_ref.shape[2]
    for line, act_ref in enumerate((near_ref, far_ref)):
        block = act_ref[...].reshape(GROUPS * SHARE, lanes).astype(jnp.float32)
        turned[line * lanes : (line + 1) * lanes, :] = block.T
    for ahead in range(4):
        owner = lax.rem(mine + ahead, 4)
        for other in range(2):
            target = core + other - 2 * core * other
            for ring in range(2):
                halves = []
                for line in range(2):
                    start = line * lanes + (ring * 2 + target) * 4 * ROWS + owner * ROWS
                    halves.append(turned[pl.ds(pl.multiple_of(start, 8), ROWS), :])
                refs[ahead][other, ring * PIECE : (ring + 1) * PIECE, :] = jnp.concatenate(halves, axis=0).astype(NARROW)


def turn(place, activations):
    tokens = GROUPS * SHARE
    lanes = 16 * ROWS
    shape = jax.ShapeDtypeStruct((2, RINGS * PIECE, tokens), NARROW)
    return pl.pallas_call(
        turn_kernel,
        out_shape=(shape,) * 4,
        grid=(RINGS // 2,),
        in_specs=[
            pl.BlockSpec(memory_space=pltpu.SMEM),
            pl.BlockSpec((GROUPS, SHARE, lanes), lambda i: (0, 0, i)),
            pl.BlockSpec((GROUPS, SHARE, lanes), lambda i: (0, 0, i + RINGS // 2)),
        ],
        out_specs=(pl.BlockSpec((2, 2 * PIECE, tokens), lambda i: (0, i, 0)),) * 4,
        scratch_shapes=[pltpu.VMEM((2 * lanes, tokens), jnp.float32)],
        compiler_params=pltpu.CompilerParams(vmem_limit_bytes=10 * MIB),
        cost_estimate=cost(3),
        name="turn",
    )(place, activations, activations)


def join_factors(factors, joined):
    @pl.when(pl.program_id(0) == 0)
    def _():
        row = 0
        for factor in factors:
            joined[row : row + factor.shape[0], :] = factor[...]
            row += factor.shape[0]
        if row < joined.shape[0]:
            joined[row:, :] = jnp.zeros((joined.shape[0] - row, joined.shape[1]), NARROW)


def multiply(rows, joined):
    return lax.dot_general(
        rows, joined[...], (((1,), (1,)), ((), ())), preferred_element_type=jnp.float32
    ).astype(NARROW)


def first_kernel(count, place_ref, *refs):
    pieces = refs[:8]
    out_ref, whole_ref, joined = refs[9 + count :]
    join_factors(refs[8 : 8 + count], joined)
    for behind in range(4):
        for across in range(2):
            source = lax.rem(place_ref[0] + 4 - behind, 4) * 2 + lax.rem(place_ref[1] + across, 2)
            lane = pl.multiple_of(source * 128, 128)
            whole_ref[:, pl.ds(lane, 128)] = pieces[behind * 2 + across][0]
    out_ref[...] = multiply(whole_ref[...], joined)


def next_kernel(count, whole_ref, *refs):
    out_ref, joined = refs[1 + count :]
    join_factors(refs[:count], joined)
    out_ref[...] = multiply(whole_ref[...], joined)


TERM_ROWS = 384


def term_call(kernel, count, rows, width, out_shape, out_specs, in_specs, operands):
    return pl.pallas_call(
        functools.partial(kernel, count),
        out_shape=out_shape,
        grid=(rows // TERM_ROWS,),
        in_specs=in_specs,
        out_specs=out_specs,
        scratch_shapes=[pltpu.VMEM((width, GROUPS * TOKENS), NARROW)],
        compiler_params=pltpu.CompilerParams(vmem_limit_bytes=18 * MIB),
        cost_estimate=cost(6),
        name="terms",
    )(*operands)


def factor_specs(factors):
    return [pl.BlockSpec(factor.shape, lambda i: (0, 0)) for factor in factors] + [pl.BlockSpec(memory_space=pl.ANY)]


def padded_width(factors):
    return -(-sum(factor.shape[0] for factor in factors) // 128) * 128


def first_terms(place, other, pieces, factors, after):
    tokens = GROUPS * TOKENS
    rows = RINGS * PIECE
    width = padded_width(factors)
    return term_call(
        first_kernel,
        len(factors),
        rows,
        width,
        (jax.ShapeDtypeStruct((rows, width), NARROW), jax.ShapeDtypeStruct((rows, tokens), NARROW)),
        (pl.BlockSpec((TERM_ROWS, width), lambda i: (i, 0)), pl.BlockSpec((TERM_ROWS, tokens), lambda i: (i, 0))),
        [pl.BlockSpec(memory_space=pltpu.SMEM)]
        + [pl.BlockSpec((1, TERM_ROWS, GROUPS * SHARE), lambda i: (other, i, 0))] * 8
        + factor_specs(factors),
        (place, *pieces, *factors, after),
    )


def next_terms(whole, factors, after):
    rows, tokens = whole.shape
    width = padded_width(factors)
    return term_call(
        next_kernel,
        len(factors),
        rows,
        width,
        jax.ShapeDtypeStruct((rows, width), NARROW),
        pl.BlockSpec((TERM_ROWS, width), lambda i: (i, 0)),
        [pl.BlockSpec((TERM_ROWS, tokens), lambda i: (i, 0))] + factor_specs(factors),
        (whole, *factors, after),
    )


def finish_kernel(place_ref, mask_ref, key_mask_ref, *refs):
    blocks = refs[:4]
    out_ref, key_out_ref = refs[4:]
    query_width = out_ref.shape[1]
    for behind in range(4):
        owner = lax.rem(place_ref[0] + behind, 4)
        rows = pl.ds(pl.multiple_of(owner * ROWS, 8), ROWS)
        total = blocks[behind][...].astype(jnp.float32) * (1.0 / LOSS_SCALE)
        out_ref[rows, :] = total[:, :query_width] * mask_ref[rows, :]
        key_out_ref[rows, :] = total[:, query_width:] * key_mask_ref[rows, :]


def finish(place, mask, key_mask, blocks):
    vmem = pl.BlockSpec(memory_space=pltpu.VMEM)
    return pl.pallas_call(
        finish_kernel,
        out_shape=(
            jax.ShapeDtypeStruct(mask.shape, jnp.float32),
            jax.ShapeDtypeStruct(key_mask.shape, jnp.float32),
        ),
        in_specs=[pl.BlockSpec(memory_space=pltpu.SMEM)] + [vmem] * 6,
        out_specs=(vmem, vmem),
        compiler_params=pltpu.CompilerParams(vmem_limit_bytes=10 * MIB),
        cost_estimate=cost(2),
        name="finish",
    )(place, mask, key_mask, *blocks)


def gate_kernel(x_ref, *refs):
    pass


def gate(x, after):
    anywhere = pl.BlockSpec(memory_space=pl.ANY)
    return pl.pallas_call(
        gate_kernel,
        out_shape=jax.ShapeDtypeStruct(x.shape, x.dtype),
        in_specs=[anywhere] * (1 + len(after)),
        out_specs=anywhere,
        input_output_aliases={0: 0},
        compiler_params=pltpu.CompilerParams(vmem_limit_bytes=MIB),
        cost_estimate=cost(0.1),
        name="gate",
    )(x, *after)


def inside_mask(latent, exponent):
    quant_step = jnp.exp2(exponent.astype(jnp.float32))
    levels = jnp.floor(latent.astype(jnp.float32) / quant_step + 0.5)
    return (jnp.abs(levels) <= 127.0).astype(jnp.float32)


def shifted(x, axis, size, by):
    return lax.ppermute(x, axis, [(at, (at + by) % size) for at in range(size)])


def load_kernel(streams, spot_ref, *refs):
    outs = refs[3 * streams :]
    for at, out_ref in enumerate(outs):
        parts = refs[3 * at : 3 * at + 3]
        total = parts[0][...].astype(jnp.float32) + parts[1][...].astype(jnp.float32)
        if len(parts[2].shape) == 2:
            total = total + parts[2][...].astype(jnp.float32)
        out_ref[...] = total.astype(NARROW)


def loads(spots, keep, got, moving):
    streams = len(moving)
    width = keep.shape[1]

    def local_spec(at):
        return pl.BlockSpec((PIECE, width), lambda i, spot: (spot[at], 0))

    whole = pl.BlockSpec((PIECE, width), lambda i, spot: (0, 0))
    in_specs = []
    operands = []
    for at, there in enumerate(moving):
        in_specs += [local_spec(at), local_spec(at)]
        operands += [keep, got]
        if there is None:
            in_specs.append(pl.BlockSpec(memory_space=pltpu.SMEM))
            operands.append(spots)
        else:
            in_specs.append(whole)
            operands.append(there)
    shape = jax.ShapeDtypeStruct((PIECE, width), NARROW)
    return pl.pallas_call(
        functools.partial(load_kernel, streams),
        out_shape=(shape,) * streams,
        grid_spec=pltpu.PrefetchScalarGridSpec(
            num_scalar_prefetch=1, grid=(1,), in_specs=in_specs, out_specs=(whole,) * streams
        ),
        compiler_params=pltpu.CompilerParams(vmem_limit_bytes=10 * MIB),
        cost_estimate=cost(2),
        name="loads",
    )(spots, *operands)


def settle_kernel(spot_ref, keep_ref, got_ref, one_ref, two_ref, mine_ref, other_ref, total):
    total[...] = (
        keep_ref[...].astype(jnp.float32)
        + got_ref[...].astype(jnp.float32)
        + one_ref[...].astype(jnp.float32)
        + two_ref[...].astype(jnp.float32)
    )
    line = spot_ref[1]
    mine_ref[...] = total[pl.ds(pl.multiple_of(line * ROWS, 8), ROWS), :].astype(NARROW)
    other_ref[...] = total[pl.ds(pl.multiple_of((1 - line) * ROWS, 8), ROWS), :].astype(NARROW)


def settle(spots, keep, got, one, two):
    width = keep.shape[1]
    local = pl.BlockSpec((PIECE, width), lambda i, spot: (spot[0], 0))
    whole = pl.BlockSpec((PIECE, width), lambda i, spot: (0, 0))
    out = pl.BlockSpec((ROWS, width), lambda i, spot: (0, 0))
    shape = jax.ShapeDtypeStruct((ROWS, width), NARROW)
    return pl.pallas_call(
        settle_kernel,
        out_shape=(shape, shape),
        grid_spec=pltpu.PrefetchScalarGridSpec(
            num_scalar_prefetch=1,
            grid=(1,),
            in_specs=[local, local, whole, whole],
            out_specs=(out, out),
            scratch_shapes=[pltpu.VMEM((PIECE, width), jnp.float32)],
        ),
        compiler_params=pltpu.CompilerParams(vmem_limit_bytes=10 * MIB),
        cost_estimate=cost(2),
        name="settle",
    )(spots, keep, got, one, two)


def merge_kernel(mine_ref, got_ref, *outs):
    total = mine_ref[...].astype(jnp.float32) + got_ref[...].astype(jnp.float32)
    for at, out_ref in enumerate(outs):
        out_ref[...] = total[:, at * WIDTH : (at + 1) * WIDTH].astype(NARROW)


def merge(mine, got):
    vmem = pl.BlockSpec(memory_space=pltpu.VMEM)
    count = mine.shape[1] // WIDTH
    return pl.pallas_call(
        merge_kernel,
        out_shape=(jax.ShapeDtypeStruct((ROWS, WIDTH), NARROW),) * count,
        in_specs=[vmem, vmem],
        out_specs=(vmem,) * count,
        compiler_params=pltpu.CompilerParams(vmem_limit_bytes=10 * MIB),
        cost_estimate=cost(1),
        name="merge",
    )(mine, got)


CHUNKS = ((0, 1), (3, 2))


def on_device(
    activations,
    w_query,
    key_weight_latent,
    query_exponent,
    key_column_exponent,
    queries,
    keys,
    teacher_attention_logits,
    document_length,
):
    place = jnp.stack([lax.axis_index("y"), lax.axis_index("xh"), lax.axis_index("core")]).astype(jnp.int32)
    ring = lax.axis_index("z")
    line = lax.axis_index("xl")
    cut = turn(place, activations)
    held = [cut[0]] + [shifted(cut[ahead], "y", 4, ahead) for ahead in (1, 2, 3)]
    swapped = [shifted(cut[0], "xh", 2, 1)]
    own = head_grads(queries, keys, teacher_attention_logits, document_length, [cut[0]])
    own = gate(own, held[1:] + swapped)
    swapped += [shifted(piece, "xh", 2, 1) for piece in held[1:]]
    pieces = []
    for pair in zip(held, swapped):
        pieces += pair
    back = shifted(own, "y", 4, 1)
    fore = shifted(own, "y", 4, 3)
    half = WIDTH // 2
    factors = [
        [own],
        [back],
        [shifted(back[:half], "y", 4, 1), shifted(fore[half:], "y", 4, 3)],
        [fore],
    ]

    mask = inside_mask(w_query, query_exponent[None, :])
    key_mask = inside_mask(key_weight_latent, key_column_exponent[None, :])

    held_terms = []
    after = place
    wholes = []
    for at, chunk in enumerate(CHUNKS):
        parts = []
        for behind in chunk:
            parts += factors[behind]
        made = []
        for other in (1, 0):
            if at == 0:
                after, whole = first_terms(place, other, pieces, parts, after)
                wholes.append(whole)
            else:
                after = next_terms(wholes[1 - other], parts, after)
            made.append(after)
        held_terms.append((made[1], shifted(made[0], "core", 2, 1)))

    def spots(*values):
        return jnp.stack([lax.rem(value + RINGS, RINGS) for value in values]).astype(jnp.int32)

    moving = [[None, None], [None, None]]
    for slot in range(4):
        for at, (keep, got) in enumerate(held_terms):
            way = 1 - 2 * at
            if slot == 0:
                (first,) = loads(spots(ring + 4 * way), keep, got, [None])
                moving[at][0] = shifted(first, "z", RINGS, way)
            else:
                left = 4 - slot
                pair = loads(spots(ring + left * way, ring - left * way), keep, got, moving[at])
                moving[at] = [shifted(pair[0], "z", RINGS, way), shifted(pair[1], "z", RINGS, -way)]
    blocks = {}
    for at, (keep, got) in enumerate(held_terms):
        mine, other = settle(jnp.stack([ring, line]).astype(jnp.int32), keep, got, *moving[at])
        parts = merge(mine, shifted(other, "xl", 2, 1))
        for behind, part in zip(CHUNKS[at], parts):
            blocks[behind] = part if behind == 0 else shifted(part, "y", 4, 4 - behind)
    return finish(place, mask, key_mask, [blocks[behind] for behind in range(4)])


def solution(mesh):
    fine = jax.sharding.Mesh(mesh.devices.reshape(2, 8, 2, 4, 2), ("xl", "z", "core", "y", "xh"))
    dp = ("xl", "z", "core")
    tensor = ("y", "xh")
    in_specs = (
        P(dp, tensor, None),
        P(dp, tensor),
        P(dp, tensor),
        P(tensor),
        P(tensor),
        P(dp, None, tensor),
        P(dp, None, tensor),
        P(dp, tensor, None, None),
        P(dp, None),
    )
    out_specs = (P(dp, tensor), P(dp, tensor))
    return jax.shard_map(on_device, mesh=fine, in_specs=in_specs, out_specs=out_specs, check_vma=False)
```

```python
import functools
import math

import jax
import jax.numpy as jnp
from jax import lax
from jax.experimental import pallas as pl
from jax.experimental.pallas import tpu as pltpu
from jax.sharding import PartitionSpec as P

SOFT_CAP = 30.0
LOSS_SCALE = 64.0
GROUPS = 2
TOKENS = 512
HEADS = 6
DIM = 96
WIDTH = 672
ROWS = 72
RINGS = 8
BAND = 128
SHARDS = 8
SHARE = 64
NARROW = jnp.bfloat16
MIB = 1024 * 1024
PIECE = 2 * ROWS
LINE_AT = 3
RING_AT = 4


def cost(time):
    return pl.CostEstimate(flops=1000, bytes_accessed=int(time * 3.5e6), transcendentals=0)


def spread_tokens(first, second):
    parts = []
    for shard in range(SHARDS):
        parts.append(first[:, shard * SHARE : (shard + 1) * SHARE])
        parts.append(second[:, shard * SHARE : (shard + 1) * SHARE])
    return jnp.concatenate(parts, axis=1).astype(NARROW)


def head_kernel(length_ref, query_ref, key_ref, teacher_ref, *refs):
    out_ref, grad_ref, query_acc, key_acc = refs[-4:]
    head = pl.program_id(0)
    group = pl.program_id(1)

    @pl.when((head == 0) & (group == 0))
    def _():
        grad_ref[...] = jnp.zeros_like(grad_ref)

    ends = [length_ref[group, 0]]
    for document in range(1, length_ref.shape[1]):
        ends.append(ends[-1] + length_ref[group, document])
    query_t = query_ref[0]
    key_t = key_ref[0]
    for first in range(0, TOKENS, BAND):
        low = max(0, first - 2 * BAND)
        high = first + BAND
        token = lax.broadcasted_iota(jnp.int32, (BAND, 1), 0) + first
        start = jnp.zeros_like(token)
        for end in ends:
            start = jnp.where(token >= end, end, start)
        column = lax.broadcasted_iota(jnp.int32, (BAND, high - low), 1) + low
        allowed = (column >= start) & (column <= token)
        dots = lax.dot_general(
            query_t[:, first : first + BAND],
            key_t[:, low:high],
            (((0,), (0,)), ((), ())),
            preferred_element_type=jnp.float32,
        )
        bent = jnp.tanh(dots * (1.0 / (math.sqrt(DIM) * SOFT_CAP)))
        student = jnp.where(allowed, jnp.exp(bent * SOFT_CAP), 0.0)
        logits = teacher_ref[0, 0, first : first + BAND, low:high].astype(jnp.float32)
        teacher = jnp.where(allowed, jnp.exp(logits), 0.0)
        student_scale = 1.0 / jnp.sum(student, axis=1, keepdims=True)
        teacher_scale = 1.0 / jnp.sum(teacher, axis=1, keepdims=True)
        scale = LOSS_SCALE / math.sqrt(DIM)
        slope = scale - scale * (bent * bent)
        grad = (student * student_scale - teacher * teacher_scale) * slope
        grad_ref[first : first + BAND, low:high] = grad.astype(NARROW)
    score_grad = grad_ref[...]
    query_grad = lax.dot_general(
        key_t, score_grad, (((1,), (1,)), ((), ())), preferred_element_type=jnp.float32
    )
    key_grad = lax.dot_general(
        query_t, score_grad, (((1,), (0,)), ((), ())), preferred_element_type=jnp.float32
    )

    @pl.when(head == 0)
    def _():
        key_acc[group] = key_grad

    @pl.when(head != 0)
    def _():
        key_acc[group] = key_acc[group] + key_grad

    @pl.when(group == 0)
    def _():
        query_acc[...] = query_grad

    @pl.when(group == GROUPS - 1)
    def _():
        out_ref[head] = spread_tokens(query_acc[...], query_grad)

    @pl.when((head == HEADS - 1) & (group == GROUPS - 1))
    def _():
        out_ref[HEADS] = spread_tokens(key_acc[0], key_acc[1])


def head_grads(queries, keys, teacher, lengths, after):
    query_t = jnp.swapaxes(queries, 1, 2)
    key_t = jnp.swapaxes(keys, 1, 2)
    shape = (HEADS + 1, DIM, GROUPS * TOKENS)
    out = pl.pallas_call(
        head_kernel,
        out_shape=jax.ShapeDtypeStruct(shape, NARROW),
        grid=(HEADS, GROUPS),
        in_specs=[
            pl.BlockSpec(memory_space=pltpu.SMEM),
            pl.BlockSpec((1, DIM, TOKENS), lambda h, g: (g, h, 0)),
            pl.BlockSpec((1, DIM, TOKENS), lambda h, g: (g, 0, 0)),
            pl.BlockSpec((1, 1, TOKENS, TOKENS), lambda h, g: (g, h, 0, 0)),
        ]
        + [pl.BlockSpec(memory_space=pl.ANY)] * len(after),
        out_specs=pl.BlockSpec(shape, lambda h, g: (0, 0, 0)),
        scratch_shapes=[
            pltpu.VMEM((TOKENS, TOKENS), NARROW),
            pltpu.VMEM((DIM, TOKENS), jnp.float32),
            pltpu.VMEM((GROUPS, DIM, TOKENS), jnp.float32),
        ],
        compiler_params=pltpu.CompilerParams(vmem_limit_bytes=12 * MIB),
        cost_estimate=cost(14),
        name="head_grads",
    )(lengths, query_t, key_t, teacher, *after)
    return out.reshape(WIDTH, GROUPS * TOKENS)


def turn_kernel(place_ref, near_ref, far_ref, *refs):
    turned = refs[4]
    mine = place_ref[0]
    core = place_ref[2]
    lanes = near_ref.shape[2]
    for line, act_ref in enumerate((near_ref, far_ref)):
        block = act_ref[...].reshape(GROUPS * SHARE, lanes).astype(jnp.float32)
        turned[line * lanes : (line + 1) * lanes, :] = block.T
    for ahead in range(4):
        owner = lax.rem(mine + ahead, 4)
        for other in range(2):
            target = core + other - 2 * core * other
            for ring in range(2):
                halves = []
                for line in range(2):
                    start = line * lanes + (ring * 2 + target) * 4 * ROWS + owner * ROWS
                    halves.append(turned[pl.ds(pl.multiple_of(start, 8), ROWS), :])
                refs[ahead][other, ring * PIECE : (ring + 1) * PIECE, :] = jnp.concatenate(halves, axis=0).astype(NARROW)


def turn(place, activations):
    tokens = GROUPS * SHARE
    lanes = 16 * ROWS
    shape = jax.ShapeDtypeStruct((2, RINGS * PIECE, tokens), NARROW)
    return pl.pallas_call(
        turn_kernel,
        out_shape=(shape,) * 4,
        grid=(RINGS // 2,),
        in_specs=[
            pl.BlockSpec(memory_space=pltpu.SMEM),
            pl.BlockSpec((GROUPS, SHARE, lanes), lambda i: (0, 0, i)),
            pl.BlockSpec((GROUPS, SHARE, lanes), lambda i: (0, 0, i + RINGS // 2)),
        ],
        out_specs=(pl.BlockSpec((2, 2 * PIECE, tokens), lambda i: (0, i, 0)),) * 4,
        scratch_shapes=[pltpu.VMEM((2 * lanes, tokens), jnp.float32)],
        compiler_params=pltpu.CompilerParams(vmem_limit_bytes=6 * MIB),
        cost_estimate=cost(3),
        name="turn",
    )(place, activations, activations)


def far_off(x):
    return pltpu.with_memory_space_constraint(x, pltpu.HBM)


def join_factors(factors, joined):
    @pl.when(pl.program_id(0) == 0)
    def _():
        row = 0
        for factor in factors:
            joined[row : row + factor.shape[0], :] = factor[...]
            row += factor.shape[0]
        if row < joined.shape[0]:
            joined[row:, :] = jnp.zeros((joined.shape[0] - row, joined.shape[1]), NARROW)


def multiply(rows, joined):
    return lax.dot_general(
        rows, joined[...], (((1,), (1,)), ((), ())), preferred_element_type=jnp.float32
    ).astype(NARROW)


def first_kernel(count, place_ref, *refs):
    pieces = refs[:8]
    out_ref, whole_ref, joined = refs[9 + count :]
    join_factors(refs[8 : 8 + count], joined)
    for behind in range(4):
        for across in range(2):
            source = lax.rem(place_ref[0] + 4 - behind, 4) * 2 + lax.rem(place_ref[1] + across, 2)
            lane = pl.multiple_of(source * 128, 128)
            whole_ref[:, pl.ds(lane, 128)] = pieces[behind * 2 + across][0]
    out_ref[...] = multiply(whole_ref[...], joined)


def next_kernel(count, whole_ref, *refs):
    out_ref, joined = refs[1 + count :]
    join_factors(refs[:count], joined)
    out_ref[...] = multiply(whole_ref[...], joined)


TERM_ROWS = 384


def term_call(kernel, count, rows, width, out_shape, out_specs, in_specs, operands):
    return pl.pallas_call(
        functools.partial(kernel, count),
        out_shape=out_shape,
        grid=(rows // TERM_ROWS,),
        in_specs=in_specs,
        out_specs=out_specs,
        scratch_shapes=[pltpu.VMEM((width, GROUPS * TOKENS), NARROW)],
        compiler_params=pltpu.CompilerParams(vmem_limit_bytes=18 * MIB),
        cost_estimate=cost(6),
        name="terms",
    )(*operands)


def factor_specs(factors):
    return [pl.BlockSpec(factor.shape, lambda i: (0, 0)) for factor in factors] + [pl.BlockSpec(memory_space=pl.ANY)]


def padded_width(factors):
    return -(-sum(factor.shape[0] for factor in factors) // 128) * 128


def first_terms(place, other, pieces, factors, after):
    tokens = GROUPS * TOKENS
    rows = RINGS * PIECE
    width = padded_width(factors)
    return term_call(
        first_kernel,
        len(factors),
        rows,
        width,
        (jax.ShapeDtypeStruct((rows, width), NARROW), jax.ShapeDtypeStruct((rows, tokens), NARROW)),
        (pl.BlockSpec((TERM_ROWS, width), lambda i: (i, 0)), pl.BlockSpec((TERM_ROWS, tokens), lambda i: (i, 0))),
        [pl.BlockSpec(memory_space=pltpu.SMEM)]
        + [pl.BlockSpec((1, TERM_ROWS, GROUPS * SHARE), lambda i: (other, i, 0))] * 8
        + factor_specs(factors),
        (place, *pieces, *factors, after),
    )


def next_terms(whole, factors, after):
    rows, tokens = whole.shape
    width = padded_width(factors)
    return term_call(
        next_kernel,
        len(factors),
        rows,
        width,
        jax.ShapeDtypeStruct((rows, width), NARROW),
        pl.BlockSpec((TERM_ROWS, width), lambda i: (i, 0)),
        [pl.BlockSpec((TERM_ROWS, tokens), lambda i: (i, 0))] + factor_specs(factors),
        (whole, *factors, after),
    )


def finish_kernel(place_ref, mask_ref, key_mask_ref, *refs):
    blocks = refs[:4]
    out_ref, key_out_ref = refs[4:]
    query_width = out_ref.shape[1]
    for behind in range(4):
        owner = lax.rem(place_ref[0] + behind, 4)
        rows = pl.ds(pl.multiple_of(owner * ROWS, 8), ROWS)
        total = blocks[behind][...].astype(jnp.float32) * (1.0 / LOSS_SCALE)
        out_ref[rows, :] = total[:, :query_width] * mask_ref[rows, :]
        key_out_ref[rows, :] = total[:, query_width:] * key_mask_ref[rows, :]


def finish(place, mask, key_mask, blocks):
    vmem = pl.BlockSpec(memory_space=pltpu.VMEM)
    return pl.pallas_call(
        finish_kernel,
        out_shape=(
            jax.ShapeDtypeStruct(mask.shape, jnp.float32),
            jax.ShapeDtypeStruct(key_mask.shape, jnp.float32),
        ),
        in_specs=[pl.BlockSpec(memory_space=pltpu.SMEM)] + [vmem] * 6,
        out_specs=(vmem, vmem),
        compiler_params=pltpu.CompilerParams(vmem_limit_bytes=6 * MIB),
        cost_estimate=cost(2),
        name="finish",
    )(place, mask, key_mask, *blocks)


def gate_kernel(x_ref, *refs):
    pass


def gate(x, after):
    anywhere = pl.BlockSpec(memory_space=pl.ANY)
    return pl.pallas_call(
        gate_kernel,
        out_shape=jax.ShapeDtypeStruct(x.shape, x.dtype),
        in_specs=[anywhere] * (1 + len(after)),
        out_specs=anywhere,
        input_output_aliases={0: 0},
        compiler_params=pltpu.CompilerParams(vmem_limit_bytes=MIB),
        cost_estimate=cost(0.1),
        name="gate",
    )(x, *after)


def inside_mask(latent, exponent):
    quant_step = jnp.exp2(exponent.astype(jnp.float32))
    levels = jnp.floor(latent.astype(jnp.float32) / quant_step + 0.5)
    return (jnp.abs(levels) <= 127.0).astype(jnp.float32)


def shifted(x, axis, size, by):
    return lax.ppermute(x, axis, [(at, (at + by) % size) for at in range(size)])


def load_kernel(streams, spot_ref, *refs):
    outs = refs[3 * streams :]
    for at, out_ref in enumerate(outs):
        parts = refs[3 * at : 3 * at + 3]
        total = parts[0][...].astype(jnp.float32) + parts[1][...].astype(jnp.float32)
        if len(parts[2].shape) == 2:
            total = total + parts[2][...].astype(jnp.float32)
        out_ref[...] = total.astype(NARROW)


def loads(place, aheads, keep, got, moving):
    streams = len(moving)
    width = keep.shape[1]

    def local_spec(at):
        return pl.BlockSpec((PIECE, width), lambda i, spot: (spot[RING_AT + aheads[at] % RINGS], 0))

    whole = pl.BlockSpec((PIECE, width), lambda i, spot: (0, 0))
    in_specs = []
    operands = []
    for at, there in enumerate(moving):
        in_specs += [local_spec(at), local_spec(at)]
        operands += [keep, got]
        if there is None:
            in_specs.append(pl.BlockSpec(memory_space=pltpu.SMEM))
            operands.append(place)
        else:
            in_specs.append(whole)
            operands.append(there)
    shape = jax.ShapeDtypeStruct((PIECE, width), NARROW)
    return pl.pallas_call(
        functools.partial(load_kernel, streams),
        out_shape=(shape,) * streams,
        grid_spec=pltpu.PrefetchScalarGridSpec(
            num_scalar_prefetch=1, grid=(1,), in_specs=in_specs, out_specs=(whole,) * streams
        ),
        compiler_params=pltpu.CompilerParams(vmem_limit_bytes=6 * MIB),
        cost_estimate=cost(2),
        name="loads",
    )(place, *operands)


def settle_kernel(spot_ref, keep_ref, got_ref, one_ref, two_ref, mine_ref, other_ref, total):
    total[...] = (
        keep_ref[...].astype(jnp.float32)
        + got_ref[...].astype(jnp.float32)
        + one_ref[...].astype(jnp.float32)
        + two_ref[...].astype(jnp.float32)
    )
    line = spot_ref[LINE_AT]
    mine_ref[...] = total[pl.ds(pl.multiple_of(line * ROWS, 8), ROWS), :].astype(NARROW)
    other_ref[...] = total[pl.ds(pl.multiple_of((1 - line) * ROWS, 8), ROWS), :].astype(NARROW)


def settle(place, keep, got, one, two):
    width = keep.shape[1]
    local = pl.BlockSpec((PIECE, width), lambda i, spot: (spot[RING_AT], 0))
    whole = pl.BlockSpec((PIECE, width), lambda i, spot: (0, 0))
    out = pl.BlockSpec((ROWS, width), lambda i, spot: (0, 0))
    shape = jax.ShapeDtypeStruct((ROWS, width), NARROW)
    return pl.pallas_call(
        settle_kernel,
        out_shape=(shape, shape),
        grid_spec=pltpu.PrefetchScalarGridSpec(
            num_scalar_prefetch=1,
            grid=(1,),
            in_specs=[local, local, whole, whole],
            out_specs=(out, out),
            scratch_shapes=[pltpu.VMEM((PIECE, width), jnp.float32)],
        ),
        compiler_params=pltpu.CompilerParams(vmem_limit_bytes=6 * MIB),
        cost_estimate=cost(2),
        name="settle",
    )(place, keep, got, one, two)


def merge_kernel(mine_ref, got_ref, *outs):
    total = mine_ref[...].astype(jnp.float32) + got_ref[...].astype(jnp.float32)
    for at, out_ref in enumerate(outs):
        out_ref[...] = total[:, at * WIDTH : (at + 1) * WIDTH].astype(NARROW)


def merge(mine, got):
    vmem = pl.BlockSpec(memory_space=pltpu.VMEM)
    count = mine.shape[1] // WIDTH
    return pl.pallas_call(
        merge_kernel,
        out_shape=(jax.ShapeDtypeStruct((ROWS, WIDTH), NARROW),) * count,
        in_specs=[vmem, vmem],
        out_specs=(vmem,) * count,
        compiler_params=pltpu.CompilerParams(vmem_limit_bytes=6 * MIB),
        cost_estimate=cost(1),
        name="merge",
    )(mine, got)


CHUNKS = ((0, 1), (3, 2))


def on_device(
    activations,
    w_query,
    key_weight_latent,
    query_exponent,
    key_column_exponent,
    queries,
    keys,
    teacher_attention_logits,
    document_length,
):
    ring = lax.axis_index("z")
    place = [lax.axis_index(axis) for axis in ("y", "xh", "core", "xl")]
    place = jnp.stack(place + [lax.rem(ring + ahead, RINGS) for ahead in range(RINGS)]).astype(jnp.int32)
    cut = turn(place, activations)
    held = [cut[0]] + [shifted(cut[ahead], "y", 4, ahead) for ahead in (1, 2, 3)]
    swapped = [shifted(cut[0], "xh", 2, 1)]
    own = head_grads(queries, keys, teacher_attention_logits, document_length, [cut[0]])
    own = gate(own, [held[1], held[3]] + swapped)
    sides = [shifted(held[ahead], "xh", 2, 1) for ahead in (1, 3)]
    swapped += [sides[0], shifted(gate(held[2], sides), "xh", 2, 1), sides[1]]
    pieces = []
    for pair in zip(held, swapped):
        pieces += pair
    back = shifted(own, "y", 4, 1)
    fore = shifted(own, "y", 4, 3)
    half = WIDTH // 2
    waited = [swapped[2]]
    factors = [
        [own],
        [back],
        [
            shifted(gate(back[:half], waited), "y", 4, 1),
            shifted(gate(fore[half:], waited), "y", 4, 3),
        ],
        [fore],
    ]

    mask = inside_mask(w_query, query_exponent[None, :])
    key_mask = inside_mask(key_weight_latent, key_column_exponent[None, :])

    held_terms = []
    after = place
    wholes = []
    for at, chunk in enumerate(CHUNKS):
        parts = []
        for behind in chunk:
            parts += factors[behind]
        made = []
        for other in (1, 0):
            if at == 0:
                after, whole = first_terms(place, other, pieces, parts, after)
                wholes.append(whole)
            else:
                after = next_terms(wholes[1 - other], parts, after)
            made.append(after)
        held_terms.append((made[1], shifted(made[0], "core", 2, 1)))

    moving = [[None, None], [None, None]]
    for slot in range(4):
        for at, (keep, got) in enumerate(held_terms):
            way = 1 - 2 * at
            if slot == 0:
                (first,) = loads(place, [4 * way], keep, got, [None])
                moving[at][0] = shifted(first, "z", RINGS, way)
            else:
                left = 4 - slot
                pair = loads(place, [left * way, -left * way], keep, got, moving[at])
                moving[at] = [shifted(pair[0], "z", RINGS, way), shifted(pair[1], "z", RINGS, -way)]
    blocks = {}
    for at, (keep, got) in enumerate(held_terms):
        mine, other = settle(place, keep, got, *moving[at])
        parts = merge(mine, shifted(other, "xl", 2, 1))
        for behind, part in zip(CHUNKS[at], parts):
            blocks[behind] = part if behind == 0 else shifted(part, "y", 4, 4 - behind)
    return finish(place, mask, key_mask, [blocks[behind] for behind in range(4)])


def solution(mesh):
    fine = jax.sharding.Mesh(mesh.devices.reshape(2, 8, 2, 4, 2), ("xl", "z", "core", "y", "xh"))
    dp = ("xl", "z", "core")
    tensor = ("y", "xh")
    in_specs = (
        P(dp, tensor, None),
        P(dp, tensor),
        P(dp, tensor),
        P(tensor),
        P(tensor),
        P(dp, None, tensor),
        P(dp, None, tensor),
        P(dp, tensor, None, None),
        P(dp, None),
    )
    out_specs = (P(dp, tensor), P(dp, tensor))
    return jax.shard_map(on_device, mesh=fine, in_specs=in_specs, out_specs=out_specs, check_vma=False)
```

```python
import functools
import math

import jax
import jax.numpy as jnp
from jax import lax
from jax.experimental import pallas as pl
from jax.experimental.pallas import tpu as pltpu
from jax.sharding import PartitionSpec as P

SOFT_CAP = 30.0
LOSS_SCALE = 64.0
GROUPS = 2
TOKENS = 512
HEADS = 6
DIM = 96
WIDTH = 672
ROWS = 72
RINGS = 8
BAND = 128
SHARDS = 8
SHARE = 64
NARROW = jnp.bfloat16
MIB = 1024 * 1024
PIECE = 2 * ROWS
LINE_AT = 3
RING_AT = 4


def cost(time):
    return pl.CostEstimate(flops=1000, bytes_accessed=int(time * 3.5e6), transcendentals=0)


def spread_tokens(first, second):
    parts = []
    for shard in range(SHARDS):
        parts.append(first[:, shard * SHARE : (shard + 1) * SHARE])
        parts.append(second[:, shard * SHARE : (shard + 1) * SHARE])
    return jnp.concatenate(parts, axis=1).astype(NARROW)


def head_kernel(length_ref, query_ref, key_ref, teacher_ref, *refs):
    out_ref, grad_ref, query_acc, key_acc = refs[-4:]
    head = pl.program_id(0)
    group = pl.program_id(1)

    @pl.when((head == 0) & (group == 0))
    def _():
        grad_ref[...] = jnp.zeros_like(grad_ref)

    ends = [length_ref[group, 0]]
    for document in range(1, length_ref.shape[1]):
        ends.append(ends[-1] + length_ref[group, document])
    query_t = query_ref[0]
    key_t = key_ref[0]
    for first in range(0, TOKENS, BAND):
        low = max(0, first - 2 * BAND)
        high = first + BAND
        token = lax.broadcasted_iota(jnp.int32, (BAND, 1), 0) + first
        start = jnp.zeros_like(token)
        for end in ends:
            start = jnp.where(token >= end, end, start)
        column = lax.broadcasted_iota(jnp.int32, (BAND, high - low), 1) + low
        allowed = (column >= start) & (column <= token)
        dots = lax.dot_general(
            query_t[:, first : first + BAND],
            key_t[:, low:high],
            (((0,), (0,)), ((), ())),
            preferred_element_type=jnp.float32,
        )
        bent = jnp.tanh(dots * (1.0 / (math.sqrt(DIM) * SOFT_CAP)))
        student = jnp.where(allowed, jnp.exp(bent * SOFT_CAP), 0.0)
        logits = teacher_ref[0, 0, first : first + BAND, low:high].astype(jnp.float32)
        teacher = jnp.where(allowed, jnp.exp(logits), 0.0)
        student_scale = 1.0 / jnp.sum(student, axis=1, keepdims=True)
        teacher_scale = 1.0 / jnp.sum(teacher, axis=1, keepdims=True)
        scale = LOSS_SCALE / math.sqrt(DIM)
        slope = scale - scale * (bent * bent)
        grad = (student * student_scale - teacher * teacher_scale) * slope
        grad_ref[first : first + BAND, low:high] = grad.astype(NARROW)
    score_grad = grad_ref[...]
    query_grad = lax.dot_general(
        key_t, score_grad, (((1,), (1,)), ((), ())), preferred_element_type=jnp.float32
    )
    key_grad = lax.dot_general(
        query_t, score_grad, (((1,), (0,)), ((), ())), preferred_element_type=jnp.float32
    )

    @pl.when(head == 0)
    def _():
        key_acc[group] = key_grad

    @pl.when(head != 0)
    def _():
        key_acc[group] = key_acc[group] + key_grad

    @pl.when(group == 0)
    def _():
        query_acc[...] = query_grad

    @pl.when(group == GROUPS - 1)
    def _():
        out_ref[head] = spread_tokens(query_acc[...], query_grad)

    @pl.when((head == HEADS - 1) & (group == GROUPS - 1))
    def _():
        out_ref[HEADS] = spread_tokens(key_acc[0], key_acc[1])


def head_grads(queries, keys, teacher, lengths, after):
    query_t = jnp.swapaxes(queries, 1, 2)
    key_t = jnp.swapaxes(keys, 1, 2)
    shape = (HEADS + 1, DIM, GROUPS * TOKENS)
    out = pl.pallas_call(
        head_kernel,
        out_shape=jax.ShapeDtypeStruct(shape, NARROW),
        grid=(HEADS, GROUPS),
        in_specs=[
            pl.BlockSpec(memory_space=pltpu.SMEM),
            pl.BlockSpec((1, DIM, TOKENS), lambda h, g: (g, h, 0)),
            pl.BlockSpec((1, DIM, TOKENS), lambda h, g: (g, 0, 0)),
            pl.BlockSpec((1, 1, TOKENS, TOKENS), lambda h, g: (g, h, 0, 0)),
        ]
        + [pl.BlockSpec(memory_space=pl.ANY)] * len(after),
        out_specs=pl.BlockSpec(shape, lambda h, g: (0, 0, 0)),
        scratch_shapes=[
            pltpu.VMEM((TOKENS, TOKENS), NARROW),
            pltpu.VMEM((DIM, TOKENS), jnp.float32),
            pltpu.VMEM((GROUPS, DIM, TOKENS), jnp.float32),
        ],
        compiler_params=pltpu.CompilerParams(vmem_limit_bytes=12 * MIB),
        cost_estimate=cost(14),
        name="head_grads",
    )(lengths, query_t, key_t, teacher, *after)
    return out.reshape(WIDTH, GROUPS * TOKENS)


def turn_kernel(place_ref, near_ref, far_ref, *refs):
    turned = refs[4]
    mine = place_ref[0]
    core = place_ref[2]
    lanes = near_ref.shape[2]
    for line, act_ref in enumerate((near_ref, far_ref)):
        block = act_ref[...].reshape(GROUPS * SHARE, lanes).astype(jnp.float32)
        turned[line * lanes : (line + 1) * lanes, :] = block.T
    for ahead in range(4):
        owner = lax.rem(mine + ahead, 4)
        for other in range(2):
            target = core + other - 2 * core * other
            for ring in range(2):
                halves = []
                for line in range(2):
                    start = line * lanes + (ring * 2 + target) * 4 * ROWS + owner * ROWS
                    halves.append(turned[pl.ds(pl.multiple_of(start, 8), ROWS), :])
                refs[ahead][other, ring * PIECE : (ring + 1) * PIECE, :] = jnp.concatenate(halves, axis=0).astype(NARROW)


def turn(place, activations):
    tokens = GROUPS * SHARE
    lanes = 16 * ROWS
    shape = jax.ShapeDtypeStruct((2, RINGS * PIECE, tokens), NARROW)
    return pl.pallas_call(
        turn_kernel,
        out_shape=(shape,) * 4,
        grid=(RINGS // 2,),
        in_specs=[
            pl.BlockSpec(memory_space=pltpu.SMEM),
            pl.BlockSpec((GROUPS, SHARE, lanes), lambda i: (0, 0, i)),
            pl.BlockSpec((GROUPS, SHARE, lanes), lambda i: (0, 0, i + RINGS // 2)),
        ],
        out_specs=(pl.BlockSpec((2, 2 * PIECE, tokens), lambda i: (0, i, 0)),) * 4,
        scratch_shapes=[pltpu.VMEM((2 * lanes, tokens), jnp.float32)],
        compiler_params=pltpu.CompilerParams(vmem_limit_bytes=6 * MIB),
        cost_estimate=cost(3),
        name="turn",
    )(place, *[pltpu.with_memory_space_constraint(activations, pltpu.HBM)] * 2)


def far_off(x):
    return pltpu.with_memory_space_constraint(x, pltpu.HBM)


def join_factors(factors, joined):
    @pl.when(pl.program_id(0) == 0)
    def _():
        row = 0
        for factor in factors:
            joined[row : row + factor.shape[0], :] = factor[...]
            row += factor.shape[0]
        if row < joined.shape[0]:
            joined[row:, :] = jnp.zeros((joined.shape[0] - row, joined.shape[1]), NARROW)


def multiply(rows, joined):
    return lax.dot_general(
        rows, joined[...], (((1,), (1,)), ((), ())), preferred_element_type=jnp.float32
    ).astype(NARROW)


def first_kernel(count, place_ref, *refs):
    pieces = refs[:8]
    out_ref, whole_ref, joined = refs[9 + count :]
    join_factors(refs[8 : 8 + count], joined)
    for behind in range(4):
        for across in range(2):
            source = lax.rem(place_ref[0] + 4 - behind, 4) * 2 + lax.rem(place_ref[1] + across, 2)
            lane = pl.multiple_of(source * 128, 128)
            whole_ref[:, pl.ds(lane, 128)] = pieces[behind * 2 + across][0]
    out_ref[...] = multiply(whole_ref[...], joined)


def next_kernel(count, whole_ref, *refs):
    out_ref, joined = refs[1 + count :]
    join_factors(refs[:count], joined)
    out_ref[...] = multiply(whole_ref[...], joined)


TERM_ROWS = 384


def term_call(kernel, count, rows, width, out_shape, out_specs, in_specs, operands):
    return pl.pallas_call(
        functools.partial(kernel, count),
        out_shape=out_shape,
        grid=(rows // TERM_ROWS,),
        in_specs=in_specs,
        out_specs=out_specs,
        scratch_shapes=[pltpu.VMEM((width, GROUPS * TOKENS), NARROW)],
        compiler_params=pltpu.CompilerParams(vmem_limit_bytes=18 * MIB),
        cost_estimate=cost(6),
        name="terms",
    )(*operands)


def factor_specs(factors):
    return [pl.BlockSpec(factor.shape, lambda i: (0, 0)) for factor in factors] + [pl.BlockSpec(memory_space=pl.ANY)]


def padded_width(factors):
    return -(-sum(factor.shape[0] for factor in factors) // 128) * 128


def first_terms(place, other, pieces, factors, after):
    tokens = GROUPS * TOKENS
    rows = RINGS * PIECE
    width = padded_width(factors)
    return term_call(
        first_kernel,
        len(factors),
        rows,
        width,
        (jax.ShapeDtypeStruct((rows, width), NARROW), jax.ShapeDtypeStruct((rows, tokens), NARROW)),
        (pl.BlockSpec((TERM_ROWS, width), lambda i: (i, 0)), pl.BlockSpec((TERM_ROWS, tokens), lambda i: (i, 0))),
        [pl.BlockSpec(memory_space=pltpu.SMEM)]
        + [pl.BlockSpec((1, TERM_ROWS, GROUPS * SHARE), lambda i: (other, i, 0))] * 8
        + factor_specs(factors),
        (place, *pieces, *factors, after),
    )


def next_terms(whole, factors, after):
    rows, tokens = whole.shape
    width = padded_width(factors)
    return term_call(
        next_kernel,
        len(factors),
        rows,
        width,
        jax.ShapeDtypeStruct((rows, width), NARROW),
        pl.BlockSpec((TERM_ROWS, width), lambda i: (i, 0)),
        [pl.BlockSpec((TERM_ROWS, tokens), lambda i: (i, 0))] + factor_specs(factors),
        (whole, *factors, after),
    )


def finish_kernel(place_ref, mask_ref, key_mask_ref, *refs):
    blocks = refs[:8]
    out_ref, key_out_ref = refs[8:]
    query_width = out_ref.shape[1]
    for behind in range(4):
        owner = lax.rem(place_ref[0] + behind, 4)
        rows = pl.ds(pl.multiple_of(owner * ROWS, 8), ROWS)
        total = blocks[2 * behind][...].astype(jnp.float32) + blocks[2 * behind + 1][...].astype(jnp.float32)
        total = total * (1.0 / LOSS_SCALE)
        out_ref[rows, :] = total[:, :query_width] * mask_ref[rows, :]
        key_out_ref[rows, :] = total[:, query_width:] * key_mask_ref[rows, :]


def finish(place, mask, key_mask, blocks):
    vmem = pl.BlockSpec(memory_space=pltpu.VMEM)
    return pl.pallas_call(
        finish_kernel,
        out_shape=(
            jax.ShapeDtypeStruct(mask.shape, jnp.float32),
            jax.ShapeDtypeStruct(key_mask.shape, jnp.float32),
        ),
        in_specs=[pl.BlockSpec(memory_space=pltpu.SMEM)] + [vmem] * 10,
        out_specs=(vmem, vmem),
        compiler_params=pltpu.CompilerParams(vmem_limit_bytes=6 * MIB),
        cost_estimate=cost(2),
        name="finish",
    )(place, mask, key_mask, *blocks)


def gate_kernel(x_ref, *refs):
    pass


def gate(x, after):
    anywhere = pl.BlockSpec(memory_space=pl.ANY)
    return pl.pallas_call(
        gate_kernel,
        out_shape=jax.ShapeDtypeStruct(x.shape, x.dtype),
        in_specs=[anywhere] * (1 + len(after)),
        out_specs=anywhere,
        input_output_aliases={0: 0},
        compiler_params=pltpu.CompilerParams(vmem_limit_bytes=MIB),
        cost_estimate=cost(0.1),
        name="gate",
    )(x, *after)


def inside_mask(latent, exponent):
    quant_step = jnp.exp2(exponent.astype(jnp.float32))
    levels = jnp.floor(latent.astype(jnp.float32) / quant_step + 0.5)
    return (jnp.abs(levels) <= 127.0).astype(jnp.float32)


def shifted(x, axis, size, by):
    return lax.ppermute(x, axis, [(at, (at + by) % size) for at in range(size)])


def load_kernel(streams, spot_ref, *refs):
    outs = refs[3 * streams :]
    for at, out_ref in enumerate(outs):
        parts = refs[3 * at : 3 * at + 3]
        total = parts[0][...].astype(jnp.float32) + parts[1][...].astype(jnp.float32)
        if len(parts[2].shape) == 2:
            total = total + parts[2][...].astype(jnp.float32)
        out_ref[...] = total.astype(NARROW)


def loads(place, aheads, keep, got, moving):
    streams = len(moving)
    width = keep.shape[1]

    def local_spec(at):
        return pl.BlockSpec((PIECE, width), lambda i, spot: (spot[RING_AT + aheads[at] % RINGS], 0))

    whole = pl.BlockSpec((PIECE, width), lambda i, spot: (0, 0))
    in_specs = []
    operands = []
    for at, there in enumerate(moving):
        in_specs += [local_spec(at), local_spec(at)]
        operands += [keep, got]
        if there is None:
            in_specs.append(pl.BlockSpec(memory_space=pltpu.SMEM))
            operands.append(place)
        else:
            in_specs.append(whole)
            operands.append(there)
    shape = jax.ShapeDtypeStruct((PIECE, width), NARROW)
    return pl.pallas_call(
        functools.partial(load_kernel, streams),
        out_shape=(shape,) * streams,
        grid_spec=pltpu.PrefetchScalarGridSpec(
            num_scalar_prefetch=1, grid=(1,), in_specs=in_specs, out_specs=(whole,) * streams
        ),
        compiler_params=pltpu.CompilerParams(vmem_limit_bytes=6 * MIB),
        cost_estimate=cost(2),
        name="loads",
    )(place, *operands)


def settle_kernel(spot_ref, keep_ref, got_ref, one_ref, two_ref, *refs):
    total = refs[-1]
    total[...] = (
        keep_ref[...].astype(jnp.float32)
        + got_ref[...].astype(jnp.float32)
        + one_ref[...].astype(jnp.float32)
        + two_ref[...].astype(jnp.float32)
    )
    line = spot_ref[LINE_AT]
    for at, start in enumerate((line, 1 - line)):
        rows = total[pl.ds(pl.multiple_of(start * ROWS, 8), ROWS), :]
        for block in range(2):
            refs[2 * at + block][...] = rows[:, block * WIDTH : (block + 1) * WIDTH].astype(NARROW)


def settle(place, keep, got, one, two):
    width = keep.shape[1]
    local = pl.BlockSpec((PIECE, width), lambda i, spot: (spot[RING_AT], 0))
    whole = pl.BlockSpec((PIECE, width), lambda i, spot: (0, 0))
    out = pl.BlockSpec((ROWS, WIDTH), lambda i, spot: (0, 0))
    shape = jax.ShapeDtypeStruct((ROWS, WIDTH), NARROW)
    return pl.pallas_call(
        settle_kernel,
        out_shape=(shape,) * 4,
        grid_spec=pltpu.PrefetchScalarGridSpec(
            num_scalar_prefetch=1,
            grid=(1,),
            in_specs=[local, local, whole, whole],
            out_specs=(out,) * 4,
            scratch_shapes=[pltpu.VMEM((PIECE, width), jnp.float32)],
        ),
        compiler_params=pltpu.CompilerParams(vmem_limit_bytes=6 * MIB),
        cost_estimate=cost(2),
        name="settle",
    )(place, keep, got, one, two)


CHUNKS = ((0, 1), (3, 2))


def on_device(
    activations,
    w_query,
    key_weight_latent,
    query_exponent,
    key_column_exponent,
    queries,
    keys,
    teacher_attention_logits,
    document_length,
):
    ring = lax.axis_index("z")
    place = [lax.axis_index(axis) for axis in ("y", "xh", "core", "xl")]
    place = jnp.stack(place + [lax.rem(ring + ahead, RINGS) for ahead in range(RINGS)]).astype(jnp.int32)
    cut = turn(place, activations)
    held = [cut[0]] + [shifted(cut[ahead], "y", 4, ahead) for ahead in (1, 2, 3)]
    swapped = [shifted(cut[0], "xh", 2, 1)]
    own = head_grads(queries, keys, teacher_attention_logits, document_length, [cut[0]])
    own = gate(own, held[1:] + swapped)
    swapped += [shifted(piece, "xh", 2, 1) for piece in held[1:]]
    pieces = []
    for pair in zip(held, swapped):
        pieces += pair
    back = shifted(own, "y", 4, 1)
    fore = shifted(own, "y", 4, 3)
    half = WIDTH // 2
    factors = [
        [own],
        [back],
        [shifted(back[:half], "y", 4, 1), shifted(fore[half:], "y", 4, 3)],
        [fore],
    ]

    mask = inside_mask(w_query, query_exponent[None, :])
    key_mask = inside_mask(key_weight_latent, key_column_exponent[None, :])

    held_terms = []
    after = fore
    wholes = []
    for at, chunk in enumerate(CHUNKS):
        parts = []
        for behind in chunk:
            parts += factors[behind]
        made = []
        for other in (1, 0):
            if at == 0:
                after, whole = first_terms(place, other, pieces, parts, after)
                wholes.append(whole)
            else:
                after = next_terms(wholes[1 - other], parts, after)
            made.append(after)
        held_terms.append((made[1], shifted(made[0], "core", 2, 1)))

    moving = [[None, None], [None, None]]
    for slot in range(4):
        for at, (keep, got) in enumerate(held_terms):
            way = 1 - 2 * at
            if slot == 0:
                (first,) = loads(place, [4 * way], keep, got, [None])
                moving[at][0] = shifted(first, "z", RINGS, way)
            else:
                left = 4 - slot
                pair = loads(place, [left * way, -left * way], keep, got, moving[at])
                moving[at] = [shifted(pair[0], "z", RINGS, way), shifted(pair[1], "z", RINGS, -way)]
    blocks = {}
    for at, (keep, got) in enumerate(held_terms):
        made = settle(place, keep, got, *moving[at])
        for behind, mine, other in zip(CHUNKS[at], made[:2], made[2:]):
            across = [(x * 4 + y, (1 - x) * 4 + (y - behind) % 4) for x in range(2) for y in range(4)]
            other = lax.ppermute(other, ("xl", "y"), across)
            blocks[behind] = (mine if behind == 0 else shifted(mine, "y", 4, 4 - behind), other)
    return finish(place, mask, key_mask, [block for behind in range(4) for block in blocks[behind]])


def solution(mesh):
    fine = jax.sharding.Mesh(mesh.devices.reshape(2, 8, 2, 4, 2), ("xl", "z", "core", "y", "xh"))
    dp = ("xl", "z", "core")
    tensor = ("y", "xh")
    in_specs = (
        P(dp, tensor, None),
        P(dp, tensor),
        P(dp, tensor),
        P(tensor),
        P(tensor),
        P(dp, None, tensor),
        P(dp, None, tensor),
        P(dp, tensor, None, None),
        P(dp, None),
    )
    out_specs = (P(dp, tensor), P(dp, tensor))
    return jax.shard_map(on_device, mesh=fine, in_specs=in_specs, out_specs=out_specs, check_vma=False)
```

```python
import functools
import math

import jax
import jax.numpy as jnp
from jax import lax
from jax.experimental import pallas as pl
from jax.experimental.pallas import tpu as pltpu
from jax.sharding import PartitionSpec as P

SOFT_CAP = 30.0
LOSS_SCALE = 64.0
GROUPS = 2
TOKENS = 512
HEADS = 6
DIM = 96
WIDTH = 672
ROWS = 72
RINGS = 8
BAND = 128
SHARDS = 8
SHARE = 64
NARROW = jnp.bfloat16
MIB = 1024 * 1024
PIECE = 2 * ROWS
LINE_AT = 3
PIECE_ORDER = (0, 1, 3, 2)
RING_AT = 4


def cost(time):
    return pl.CostEstimate(flops=1000, bytes_accessed=int(time * 3.5e6), transcendentals=0)


def spread_tokens(first, second):
    parts = []
    for shard in range(SHARDS):
        parts.append(first[:, shard * SHARE : (shard + 1) * SHARE])
        parts.append(second[:, shard * SHARE : (shard + 1) * SHARE])
    return jnp.concatenate(parts, axis=1).astype(NARROW)


def head_kernel(length_ref, query_ref, key_ref, teacher_ref, *refs):
    out_ref, grad_ref, query_acc, key_acc = refs[-4:]
    head = pl.program_id(0)
    group = pl.program_id(1)

    @pl.when((head == 0) & (group == 0))
    def _():
        grad_ref[...] = jnp.zeros_like(grad_ref)

    ends = [length_ref[group, 0]]
    for document in range(1, length_ref.shape[1]):
        ends.append(ends[-1] + length_ref[group, document])
    query_t = query_ref[0]
    key_t = key_ref[0]
    for first in range(0, TOKENS, BAND):
        low = max(0, first - 2 * BAND)
        high = first + BAND
        token = lax.broadcasted_iota(jnp.int32, (BAND, 1), 0) + first
        start = jnp.zeros_like(token)
        for end in ends:
            start = jnp.where(token >= end, end, start)
        column = lax.broadcasted_iota(jnp.int32, (BAND, high - low), 1) + low
        allowed = (column >= start) & (column <= token)
        dots = lax.dot_general(
            query_t[:, first : first + BAND],
            key_t[:, low:high],
            (((0,), (0,)), ((), ())),
            preferred_element_type=jnp.float32,
        )
        bent = jnp.tanh(dots * (1.0 / (math.sqrt(DIM) * SOFT_CAP)))
        student = jnp.where(allowed, jnp.exp(bent * SOFT_CAP), 0.0)
        logits = teacher_ref[0, 0, first : first + BAND, low:high].astype(jnp.float32)
        teacher = jnp.where(allowed, jnp.exp(logits), 0.0)
        student_scale = 1.0 / jnp.sum(student, axis=1, keepdims=True)
        teacher_scale = 1.0 / jnp.sum(teacher, axis=1, keepdims=True)
        scale = LOSS_SCALE / math.sqrt(DIM)
        slope = scale - scale * (bent * bent)
        grad = (student * student_scale - teacher * teacher_scale) * slope
        grad_ref[first : first + BAND, low:high] = grad.astype(NARROW)
    score_grad = grad_ref[...]
    query_grad = lax.dot_general(
        key_t, score_grad, (((1,), (1,)), ((), ())), preferred_element_type=jnp.float32
    )
    key_grad = lax.dot_general(
        query_t, score_grad, (((1,), (0,)), ((), ())), preferred_element_type=jnp.float32
    )

    @pl.when(head == 0)
    def _():
        key_acc[group] = key_grad

    @pl.when(head != 0)
    def _():
        key_acc[group] = key_acc[group] + key_grad

    @pl.when(group == 0)
    def _():
        query_acc[...] = query_grad

    @pl.when(group == GROUPS - 1)
    def _():
        out_ref[head] = spread_tokens(query_acc[...], query_grad)

    @pl.when((head == HEADS - 1) & (group == GROUPS - 1))
    def _():
        out_ref[HEADS] = spread_tokens(key_acc[0], key_acc[1])


def head_grads(queries, keys, teacher, lengths, after):
    query_t = jnp.swapaxes(queries, 1, 2)
    key_t = jnp.swapaxes(keys, 1, 2)
    shape = (HEADS + 1, DIM, GROUPS * TOKENS)
    out = pl.pallas_call(
        head_kernel,
        out_shape=jax.ShapeDtypeStruct(shape, NARROW),
        grid=(HEADS, GROUPS),
        in_specs=[
            pl.BlockSpec(memory_space=pltpu.SMEM),
            pl.BlockSpec((1, DIM, TOKENS), lambda h, g: (g, h, 0)),
            pl.BlockSpec((1, DIM, TOKENS), lambda h, g: (g, 0, 0)),
            pl.BlockSpec((1, 1, TOKENS, TOKENS), lambda h, g: (g, h, 0, 0)),
        ]
        + [pl.BlockSpec(memory_space=pl.ANY)] * len(after),
        out_specs=pl.BlockSpec(shape, lambda h, g: (0, 0, 0)),
        scratch_shapes=[
            pltpu.VMEM((TOKENS, TOKENS), NARROW),
            pltpu.VMEM((DIM, TOKENS), jnp.float32),
            pltpu.VMEM((GROUPS, DIM, TOKENS), jnp.float32),
        ],
        compiler_params=pltpu.CompilerParams(vmem_limit_bytes=12 * MIB),
        cost_estimate=cost(14),
        name="head_grads",
    )(lengths, query_t, key_t, teacher, *after)
    return out.reshape(WIDTH, GROUPS * TOKENS)


def turn_kernel(place_ref, near_ref, far_ref, *refs):
    turned = refs[4]
    mine = place_ref[0]
    core = place_ref[2]
    lanes = near_ref.shape[2]
    for line, act_ref in enumerate((near_ref, far_ref)):
        block = act_ref[...].reshape(GROUPS * SHARE, lanes).astype(jnp.float32)
        turned[line * lanes : (line + 1) * lanes, :] = block.T
    for ahead in range(4):
        owner = lax.rem(mine + ahead, 4)
        for other in range(2):
            target = core + other - 2 * core * other
            for ring in range(2):
                halves = []
                for line in range(2):
                    start = line * lanes + (ring * 2 + target) * 4 * ROWS + owner * ROWS
                    halves.append(turned[pl.ds(pl.multiple_of(start, 8), ROWS), :])
                refs[ahead][other, ring * PIECE : (ring + 1) * PIECE, :] = jnp.concatenate(halves, axis=0).astype(NARROW)


def turn(place, activations):
    tokens = GROUPS * SHARE
    lanes = 16 * ROWS
    shape = jax.ShapeDtypeStruct((2, RINGS * PIECE, tokens), NARROW)
    return pl.pallas_call(
        turn_kernel,
        out_shape=(shape,) * 4,
        grid=(RINGS // 2,),
        in_specs=[
            pl.BlockSpec(memory_space=pltpu.SMEM),
            pl.BlockSpec((GROUPS, SHARE, lanes), lambda i: (0, 0, i)),
            pl.BlockSpec((GROUPS, SHARE, lanes), lambda i: (0, 0, i + RINGS // 2)),
        ],
        out_specs=(pl.BlockSpec((2, 2 * PIECE, tokens), lambda i: (0, i, 0)),) * 4,
        scratch_shapes=[pltpu.VMEM((2 * lanes, tokens), jnp.float32)],
        compiler_params=pltpu.CompilerParams(vmem_limit_bytes=6 * MIB),
        cost_estimate=cost(3),
        name="turn",
    )(place, *[pltpu.with_memory_space_constraint(activations, pltpu.HBM)] * 2)


def far_off(x):
    return pltpu.with_memory_space_constraint(x, pltpu.HBM)


def join_factors(factors, joined):
    @pl.when(pl.program_id(0) == 0)
    def _():
        row = 0
        for factor in factors:
            joined[row : row + factor.shape[0], :] = factor[...]
            row += factor.shape[0]
        if row < joined.shape[0]:
            joined[row:, :] = jnp.zeros((joined.shape[0] - row, joined.shape[1]), NARROW)


def multiply(rows, joined):
    return lax.dot_general(
        rows, joined[...], (((1,), (1,)), ((), ())), preferred_element_type=jnp.float32
    ).astype(NARROW)


def first_kernel(count, place_ref, *refs):
    pieces = refs[:8]
    out_ref, whole_ref, joined = refs[9 + count :]
    join_factors(refs[8 : 8 + count], joined)
    for at, behind in enumerate(PIECE_ORDER):
        for across in range(2):
            source = lax.rem(place_ref[0] + 4 - behind, 4) * 2 + lax.rem(place_ref[1] + across, 2)
            lane = pl.multiple_of(source * 128, 128)
            whole_ref[:, pl.ds(lane, 128)] = pieces[at * 2 + across][0]
    out_ref[...] = multiply(whole_ref[...], joined)


def next_kernel(count, whole_ref, *refs):
    out_ref, joined = refs[1 + count :]
    join_factors(refs[:count], joined)
    out_ref[...] = multiply(whole_ref[...], joined)


TERM_ROWS = 384


def term_call(kernel, count, rows, width, out_shape, out_specs, in_specs, operands):
    return pl.pallas_call(
        functools.partial(kernel, count),
        out_shape=out_shape,
        grid=(rows // TERM_ROWS,),
        in_specs=in_specs,
        out_specs=out_specs,
        scratch_shapes=[pltpu.VMEM((width, GROUPS * TOKENS), NARROW)],
        compiler_params=pltpu.CompilerParams(vmem_limit_bytes=18 * MIB),
        cost_estimate=cost(6),
        name="terms",
    )(*operands)


def factor_specs(factors):
    return [pl.BlockSpec(factor.shape, lambda i: (0, 0)) for factor in factors] + [pl.BlockSpec(memory_space=pl.ANY)]


def padded_width(factors):
    return -(-sum(factor.shape[0] for factor in factors) // 128) * 128


def first_terms(place, other, pieces, factors, after):
    tokens = GROUPS * TOKENS
    rows = RINGS * PIECE
    width = padded_width(factors)
    return term_call(
        first_kernel,
        len(factors),
        rows,
        width,
        (jax.ShapeDtypeStruct((rows, width), NARROW), jax.ShapeDtypeStruct((rows, tokens), NARROW)),
        (pl.BlockSpec((TERM_ROWS, width), lambda i: (i, 0)), pl.BlockSpec((TERM_ROWS, tokens), lambda i: (i, 0))),
        [pl.BlockSpec(memory_space=pltpu.SMEM)]
        + [pl.BlockSpec((1, TERM_ROWS, GROUPS * SHARE), lambda i: (other, i, 0))] * 8
        + factor_specs(factors),
        (place, *pieces, *factors, after),
    )


def next_terms(whole, factors, after):
    rows, tokens = whole.shape
    width = padded_width(factors)
    return term_call(
        next_kernel,
        len(factors),
        rows,
        width,
        jax.ShapeDtypeStruct((rows, width), NARROW),
        pl.BlockSpec((TERM_ROWS, width), lambda i: (i, 0)),
        [pl.BlockSpec((TERM_ROWS, tokens), lambda i: (i, 0))] + factor_specs(factors),
        (whole, *factors, after),
    )


def finish_kernel(place_ref, mask_ref, key_mask_ref, *refs):
    blocks = refs[:8]
    out_ref, key_out_ref = refs[8:]
    query_width = out_ref.shape[1]
    for behind in range(4):
        owner = lax.rem(place_ref[0] + behind, 4)
        rows = pl.ds(pl.multiple_of(owner * ROWS, 8), ROWS)
        total = blocks[2 * behind][...].astype(jnp.float32) + blocks[2 * behind + 1][...].astype(jnp.float32)
        total = total * (1.0 / LOSS_SCALE)
        out_ref[rows, :] = total[:, :query_width] * mask_ref[rows, :]
        key_out_ref[rows, :] = total[:, query_width:] * key_mask_ref[rows, :]


def finish(place, mask, key_mask, blocks):
    vmem = pl.BlockSpec(memory_space=pltpu.VMEM)
    return pl.pallas_call(
        finish_kernel,
        out_shape=(
            jax.ShapeDtypeStruct(mask.shape, jnp.float32),
            jax.ShapeDtypeStruct(key_mask.shape, jnp.float32),
        ),
        in_specs=[pl.BlockSpec(memory_space=pltpu.SMEM)] + [vmem] * 10,
        out_specs=(vmem, vmem),
        compiler_params=pltpu.CompilerParams(vmem_limit_bytes=6 * MIB),
        cost_estimate=cost(2),
        name="finish",
    )(place, mask, key_mask, *blocks)


def gate_kernel(x_ref, *refs):
    pass


def gate(x, after):
    anywhere = pl.BlockSpec(memory_space=pl.ANY)
    return pl.pallas_call(
        gate_kernel,
        out_shape=jax.ShapeDtypeStruct(x.shape, x.dtype),
        in_specs=[anywhere] * (1 + len(after)),
        out_specs=anywhere,
        input_output_aliases={0: 0},
        compiler_params=pltpu.CompilerParams(vmem_limit_bytes=MIB),
        cost_estimate=cost(0.1),
        name="gate",
    )(x, *after)


def inside_mask(latent, exponent):
    quant_step = jnp.exp2(exponent.astype(jnp.float32))
    levels = jnp.floor(latent.astype(jnp.float32) / quant_step + 0.5)
    return (jnp.abs(levels) <= 127.0).astype(jnp.float32)


def shifted(x, axis, size, by):
    return lax.ppermute(x, axis, [(at, (at + by) % size) for at in range(size)])


def load_kernel(streams, spot_ref, *refs):
    outs = refs[3 * streams :]
    for at, out_ref in enumerate(outs):
        parts = refs[3 * at : 3 * at + 3]
        total = parts[0][...].astype(jnp.float32) + parts[1][...].astype(jnp.float32)
        if len(parts[2].shape) == 2:
            total = total + parts[2][...].astype(jnp.float32)
        out_ref[...] = total.astype(NARROW)


def loads(place, aheads, keep, got, moving):
    streams = len(moving)
    width = keep.shape[1]

    def local_spec(at):
        return pl.BlockSpec((PIECE, width), lambda i, spot: (spot[RING_AT + aheads[at] % RINGS], 0))

    whole = pl.BlockSpec((PIECE, width), lambda i, spot: (0, 0))
    in_specs = []
    operands = []
    for at, there in enumerate(moving):
        in_specs += [local_spec(at), local_spec(at)]
        operands += [keep, got]
        if there is None:
            in_specs.append(pl.BlockSpec(memory_space=pltpu.SMEM))
            operands.append(place)
        else:
            in_specs.append(whole)
            operands.append(there)
    shape = jax.ShapeDtypeStruct((PIECE, width), NARROW)
    return pl.pallas_call(
        functools.partial(load_kernel, streams),
        out_shape=(shape,) * streams,
        grid_spec=pltpu.PrefetchScalarGridSpec(
            num_scalar_prefetch=1, grid=(1,), in_specs=in_specs, out_specs=(whole,) * streams
        ),
        compiler_params=pltpu.CompilerParams(vmem_limit_bytes=6 * MIB),
        cost_estimate=cost(2),
        name="loads",
    )(place, *operands)


def settle_kernel(spot_ref, keep_ref, got_ref, one_ref, two_ref, *refs):
    total = refs[-1]
    total[...] = (
        keep_ref[...].astype(jnp.float32)
        + got_ref[...].astype(jnp.float32)
        + one_ref[...].astype(jnp.float32)
        + two_ref[...].astype(jnp.float32)
    )
    line = spot_ref[LINE_AT]
    for at, start in enumerate((line, 1 - line)):
        rows = total[pl.ds(pl.multiple_of(start * ROWS, 8), ROWS), :]
        for block in range(2):
            refs[2 * at + block][...] = rows[:, block * WIDTH : (block + 1) * WIDTH].astype(NARROW)


def settle(place, keep, got, one, two):
    width = keep.shape[1]
    local = pl.BlockSpec((PIECE, width), lambda i, spot: (spot[RING_AT], 0))
    whole = pl.BlockSpec((PIECE, width), lambda i, spot: (0, 0))
    out = pl.BlockSpec((ROWS, WIDTH), lambda i, spot: (0, 0))
    shape = jax.ShapeDtypeStruct((ROWS, WIDTH), NARROW)
    return pl.pallas_call(
        settle_kernel,
        out_shape=(shape,) * 4,
        grid_spec=pltpu.PrefetchScalarGridSpec(
            num_scalar_prefetch=1,
            grid=(1,),
            in_specs=[local, local, whole, whole],
            out_specs=(out,) * 4,
            scratch_shapes=[pltpu.VMEM((PIECE, width), jnp.float32)],
        ),
        compiler_params=pltpu.CompilerParams(vmem_limit_bytes=6 * MIB),
        cost_estimate=cost(2),
        name="settle",
    )(place, keep, got, one, two)


CHUNKS = ((1, 3), (2, 0))


def on_device(
    activations,
    w_query,
    key_weight_latent,
    query_exponent,
    key_column_exponent,
    queries,
    keys,
    teacher_attention_logits,
    document_length,
):
    ring = lax.axis_index("z")
    place = [lax.axis_index(axis) for axis in ("y", "xh", "core", "xl")]
    place = jnp.stack(place + [lax.rem(ring + ahead, RINGS) for ahead in range(RINGS)]).astype(jnp.int32)
    cut = turn(place, activations)
    held = [cut[0]] + [shifted(cut[ahead], "y", 4, ahead) for ahead in PIECE_ORDER[1:]]
    swapped = [shifted(cut[0], "xh", 2, 1)]
    own = head_grads(queries, keys, teacher_attention_logits, document_length, [cut[0]])
    own = gate(own, held[1:] + swapped)
    swapped += [shifted(piece, "xh", 2, 1) for piece in held[1:]]
    pieces = []
    for pair in zip(held, swapped):
        pieces += pair
    back = shifted(own, "y", 4, 1)
    fore = shifted(own, "y", 4, 3)
    half = WIDTH // 2
    factors = [
        [own],
        [back],
        [shifted(back[:half], "y", 4, 1), shifted(fore[half:], "y", 4, 3)],
        [fore],
    ]

    mask = inside_mask(w_query, query_exponent[None, :])
    key_mask = inside_mask(key_weight_latent, key_column_exponent[None, :])

    held_terms = []
    after = fore
    wholes = []
    for at, chunk in enumerate(CHUNKS):
        parts = []
        for behind in chunk:
            parts += factors[behind]
        made = []
        for other in (1, 0):
            if at == 0:
                after, whole = first_terms(place, other, pieces, parts, after)
                wholes.append(whole)
            else:
                after = next_terms(wholes[1 - other], parts, after)
            made.append(after)
        held_terms.append((made[1], shifted(made[0], "core", 2, 1)))

    moving = [[None, None], [None, None]]
    for slot in range(4):
        for at, (keep, got) in enumerate(held_terms):
            way = 1 - 2 * at
            aheads = [(4 - slot) * way, (slot - 3) * way]
            count = 2 if slot < 3 else 1
            sums = loads(place, aheads[:count], keep, got, moving[at][:count])
            for stream, load in enumerate(sums):
                moving[at][stream] = shifted(load, "z", RINGS, -way if stream else way)
    blocks = {}
    for at, (keep, got) in enumerate(held_terms):
        made = settle(place, keep, got, *moving[at])
        for behind, mine, other in zip(CHUNKS[at], made[:2], made[2:]):
            across = [(x * 4 + y, (1 - x) * 4 + (y - behind) % 4) for x in range(2) for y in range(4)]
            other = lax.ppermute(other, ("xl", "y"), across)
            blocks[behind] = (mine if behind == 0 else shifted(mine, "y", 4, 4 - behind), other)
    return finish(place, mask, key_mask, [block for behind in range(4) for block in blocks[behind]])


def solution(mesh):
    fine = jax.sharding.Mesh(mesh.devices.reshape(2, 8, 2, 4, 2), ("xl", "z", "core", "y", "xh"))
    dp = ("xl", "z", "core")
    tensor = ("y", "xh")
    in_specs = (
        P(dp, tensor, None),
        P(dp, tensor),
        P(dp, tensor),
        P(tensor),
        P(tensor),
        P(dp, None, tensor),
        P(dp, None, tensor),
        P(dp, tensor, None, None),
        P(dp, None),
    )
    out_specs = (P(dp, tensor), P(dp, tensor))
    return jax.shard_map(on_device, mesh=fine, in_specs=in_specs, out_specs=out_specs, check_vma=False)
```

```python
import functools
import math

import jax
import jax.numpy as jnp
from jax import lax
from jax.experimental import pallas as pl
from jax.experimental.pallas import tpu as pltpu
from jax.sharding import PartitionSpec as P

SOFT_CAP = 30.0
LOSS_SCALE = 64.0
GROUPS = 2
TOKENS = 512
HEADS = 6
DIM = 96
WIDTH = 672
ROWS = 72
RINGS = 8
BAND = 128
SHARDS = 8
SHARE = 64
NARROW = jnp.bfloat16
MIB = 1024 * 1024
PIECE = 2 * ROWS
LINE_AT = 3
PIECE_ORDER = (0, 1, 3, 2)
RING_AT = 4


def cost(time):
    return pl.CostEstimate(flops=1000, bytes_accessed=int(time * 3.5e6), transcendentals=0)


def spread_tokens(first, second):
    parts = []
    for shard in range(SHARDS):
        parts.append(first[:, shard * SHARE : (shard + 1) * SHARE])
        parts.append(second[:, shard * SHARE : (shard + 1) * SHARE])
    return jnp.concatenate(parts, axis=1).astype(NARROW)


def head_kernel(length_ref, query_ref, key_ref, teacher_ref, *refs):
    out_ref, grad_ref, query_acc, key_acc = refs[-4:]
    head = pl.program_id(0)
    group = pl.program_id(1)

    @pl.when((head == 0) & (group == 0))
    def _():
        grad_ref[...] = jnp.zeros_like(grad_ref)

    ends = [length_ref[group, 0]]
    for document in range(1, length_ref.shape[1]):
        ends.append(ends[-1] + length_ref[group, document])
    query_t = query_ref[0]
    key_t = key_ref[0]
    for first in range(0, TOKENS, BAND):
        low = max(0, first - 2 * BAND)
        high = first + BAND
        token = lax.broadcasted_iota(jnp.int32, (BAND, 1), 0) + first
        start = jnp.zeros_like(token)
        for end in ends:
            start = jnp.where(token >= end, end, start)
        column = lax.broadcasted_iota(jnp.int32, (BAND, high - low), 1) + low
        allowed = (column >= start) & (column <= token)
        dots = lax.dot_general(
            query_t[:, first : first + BAND],
            key_t[:, low:high],
            (((0,), (0,)), ((), ())),
            preferred_element_type=jnp.float32,
        )
        bent = jnp.tanh(dots * (1.0 / (math.sqrt(DIM) * SOFT_CAP)))
        student = jnp.where(allowed, jnp.exp(bent * SOFT_CAP), 0.0)
        logits = teacher_ref[0, 0, first : first + BAND, low:high].astype(jnp.float32)
        teacher = jnp.where(allowed, jnp.exp(logits), 0.0)
        student_scale = 1.0 / jnp.sum(student, axis=1, keepdims=True)
        teacher_scale = 1.0 / jnp.sum(teacher, axis=1, keepdims=True)
        scale = LOSS_SCALE / math.sqrt(DIM)
        slope = scale - scale * (bent * bent)
        grad = (student * student_scale - teacher * teacher_scale) * slope
        grad_ref[first : first + BAND, low:high] = grad.astype(NARROW)
    score_grad = grad_ref[...]
    query_grad = lax.dot_general(
        key_t, score_grad, (((1,), (1,)), ((), ())), preferred_element_type=jnp.float32
    )
    key_grad = lax.dot_general(
        query_t, score_grad, (((1,), (0,)), ((), ())), preferred_element_type=jnp.float32
    )

    @pl.when(head == 0)
    def _():
        key_acc[group] = key_grad

    @pl.when(head != 0)
    def _():
        key_acc[group] = key_acc[group] + key_grad

    @pl.when(group == 0)
    def _():
        query_acc[...] = query_grad

    @pl.when(group == GROUPS - 1)
    def _():
        out_ref[head] = spread_tokens(query_acc[...], query_grad)

    @pl.when((head == HEADS - 1) & (group == GROUPS - 1))
    def _():
        out_ref[HEADS] = spread_tokens(key_acc[0], key_acc[1])


def head_grads(queries, keys, teacher, lengths, after):
    query_t = jnp.swapaxes(queries, 1, 2)
    key_t = jnp.swapaxes(keys, 1, 2)
    shape = (HEADS + 1, DIM, GROUPS * TOKENS)
    out = pl.pallas_call(
        head_kernel,
        out_shape=jax.ShapeDtypeStruct(shape, NARROW),
        grid=(HEADS, GROUPS),
        in_specs=[
            pl.BlockSpec(memory_space=pltpu.SMEM),
            pl.BlockSpec((1, DIM, TOKENS), lambda h, g: (g, h, 0)),
            pl.BlockSpec((1, DIM, TOKENS), lambda h, g: (g, 0, 0)),
            pl.BlockSpec((1, 1, TOKENS, TOKENS), lambda h, g: (g, h, 0, 0)),
        ]
        + [pl.BlockSpec(memory_space=pl.ANY)] * len(after),
        out_specs=pl.BlockSpec(shape, lambda h, g: (0, 0, 0)),
        scratch_shapes=[
            pltpu.VMEM((TOKENS, TOKENS), NARROW),
            pltpu.VMEM((DIM, TOKENS), jnp.float32),
            pltpu.VMEM((GROUPS, DIM, TOKENS), jnp.float32),
        ],
        compiler_params=pltpu.CompilerParams(vmem_limit_bytes=12 * MIB),
        cost_estimate=cost(14),
        name="head_grads",
    )(lengths, query_t, key_t, teacher, *after)
    return out.reshape(WIDTH, GROUPS * TOKENS)


def turn_kernel(place_ref, near_ref, far_ref, *refs):
    turned = refs[4]
    mine = place_ref[0]
    core = place_ref[2]
    lanes = near_ref.shape[2]
    for line, act_ref in enumerate((near_ref, far_ref)):
        block = act_ref[...].reshape(GROUPS * SHARE, lanes).astype(jnp.float32)
        turned[line * lanes : (line + 1) * lanes, :] = block.T
    for ahead in range(4):
        owner = lax.rem(mine + ahead, 4)
        for other in range(2):
            target = core + other - 2 * core * other
            for ring in range(2):
                halves = []
                for line in range(2):
                    start = line * lanes + (ring * 2 + target) * 4 * ROWS + owner * ROWS
                    halves.append(turned[pl.ds(pl.multiple_of(start, 8), ROWS), :])
                refs[ahead][other, ring * PIECE : (ring + 1) * PIECE, :] = jnp.concatenate(halves, axis=0).astype(NARROW)


def turn(place, activations):
    tokens = GROUPS * SHARE
    lanes = 16 * ROWS
    shape = jax.ShapeDtypeStruct((2, RINGS * PIECE, tokens), NARROW)
    return pl.pallas_call(
        turn_kernel,
        out_shape=(shape,) * 4,
        grid=(RINGS // 2,),
        in_specs=[
            pl.BlockSpec(memory_space=pltpu.SMEM),
            pl.BlockSpec((GROUPS, SHARE, lanes), lambda i: (0, 0, i)),
            pl.BlockSpec((GROUPS, SHARE, lanes), lambda i: (0, 0, i + RINGS // 2)),
        ],
        out_specs=(pl.BlockSpec((2, 2 * PIECE, tokens), lambda i: (0, i, 0)),) * 4,
        scratch_shapes=[pltpu.VMEM((2 * lanes, tokens), jnp.float32)],
        compiler_params=pltpu.CompilerParams(vmem_limit_bytes=6 * MIB),
        cost_estimate=cost(3),
        name="turn",
    )(place, *[pltpu.with_memory_space_constraint(activations, pltpu.HBM)] * 2)


def far_off(x):
    return pltpu.with_memory_space_constraint(x, pltpu.HBM)


def join_factors(factors, joined):
    @pl.when(pl.program_id(0) == 0)
    def _():
        row = 0
        for factor in factors:
            joined[row : row + factor.shape[0], :] = factor[...]
            row += factor.shape[0]
        if row < joined.shape[0]:
            joined[row:, :] = jnp.zeros((joined.shape[0] - row, joined.shape[1]), NARROW)


def multiply(rows, joined):
    return lax.dot_general(
        rows, joined[...], (((1,), (1,)), ((), ())), preferred_element_type=jnp.float32
    ).astype(NARROW)


def first_kernel(count, place_ref, *refs):
    pieces = refs[:8]
    out_ref, whole_ref, joined = refs[9 + count :]
    join_factors(refs[8 : 8 + count], joined)
    for at, behind in enumerate(PIECE_ORDER):
        for across in range(2):
            source = lax.rem(place_ref[0] + 4 - behind, 4) * 2 + lax.rem(place_ref[1] + across, 2)
            lane = pl.multiple_of(source * 128, 128)
            whole_ref[:, pl.ds(lane, 128)] = pieces[at + 4 * across][0]
    out_ref[...] = multiply(whole_ref[...], joined)


def next_kernel(count, whole_ref, *refs):
    out_ref, joined = refs[1 + count :]
    join_factors(refs[:count], joined)
    out_ref[...] = multiply(whole_ref[...], joined)


TERM_ROWS = 384


def term_call(kernel, count, rows, width, out_shape, out_specs, in_specs, operands):
    return pl.pallas_call(
        functools.partial(kernel, count),
        out_shape=out_shape,
        grid=(rows // TERM_ROWS,),
        in_specs=in_specs,
        out_specs=out_specs,
        scratch_shapes=[pltpu.VMEM((width, GROUPS * TOKENS), NARROW)],
        compiler_params=pltpu.CompilerParams(vmem_limit_bytes=18 * MIB),
        cost_estimate=cost(6),
        name="terms",
    )(*operands)


def factor_specs(factors):
    return [pl.BlockSpec(factor.shape, lambda i: (0, 0)) for factor in factors] + [pl.BlockSpec(memory_space=pl.ANY)]


def padded_width(factors):
    return -(-sum(factor.shape[0] for factor in factors) // 128) * 128


def first_terms(place, other, pieces, factors, after):
    tokens = GROUPS * TOKENS
    rows = RINGS * PIECE
    width = padded_width(factors)
    return term_call(
        first_kernel,
        len(factors),
        rows,
        width,
        (jax.ShapeDtypeStruct((rows, width), NARROW), jax.ShapeDtypeStruct((rows, tokens), NARROW)),
        (pl.BlockSpec((TERM_ROWS, width), lambda i: (i, 0)), pl.BlockSpec((TERM_ROWS, tokens), lambda i: (i, 0))),
        [pl.BlockSpec(memory_space=pltpu.SMEM)]
        + [pl.BlockSpec((1, TERM_ROWS, GROUPS * SHARE), lambda i: (other, i, 0))] * 8
        + factor_specs(factors),
        (place, *pieces, *factors, after),
    )


def next_terms(whole, factors, after):
    rows, tokens = whole.shape
    width = padded_width(factors)
    return term_call(
        next_kernel,
        len(factors),
        rows,
        width,
        jax.ShapeDtypeStruct((rows, width), NARROW),
        pl.BlockSpec((TERM_ROWS, width), lambda i: (i, 0)),
        [pl.BlockSpec((TERM_ROWS, tokens), lambda i: (i, 0))] + factor_specs(factors),
        (whole, *factors, after),
    )


def finish_kernel(place_ref, mask_ref, key_mask_ref, *refs):
    blocks = refs[:8]
    out_ref, key_out_ref = refs[8:]
    query_width = out_ref.shape[1]
    for behind in range(4):
        owner = lax.rem(place_ref[0] + behind, 4)
        rows = pl.ds(pl.multiple_of(owner * ROWS, 8), ROWS)
        total = blocks[2 * behind][...].astype(jnp.float32) + blocks[2 * behind + 1][...].astype(jnp.float32)
        total = total * (1.0 / LOSS_SCALE)
        out_ref[rows, :] = total[:, :query_width] * mask_ref[rows, :]
        key_out_ref[rows, :] = total[:, query_width:] * key_mask_ref[rows, :]


def finish(place, mask, key_mask, blocks):
    vmem = pl.BlockSpec(memory_space=pltpu.VMEM)
    return pl.pallas_call(
        finish_kernel,
        out_shape=(
            jax.ShapeDtypeStruct(mask.shape, jnp.float32),
            jax.ShapeDtypeStruct(key_mask.shape, jnp.float32),
        ),
        in_specs=[pl.BlockSpec(memory_space=pltpu.SMEM)] + [vmem] * 10,
        out_specs=(vmem, vmem),
        compiler_params=pltpu.CompilerParams(vmem_limit_bytes=6 * MIB),
        cost_estimate=cost(2),
        name="finish",
    )(place, mask, key_mask, *blocks)


def gate_kernel(x_ref, *refs):
    pass


def gate(x, after):
    anywhere = pl.BlockSpec(memory_space=pl.ANY)
    return pl.pallas_call(
        gate_kernel,
        out_shape=jax.ShapeDtypeStruct(x.shape, x.dtype),
        in_specs=[anywhere] * (1 + len(after)),
        out_specs=anywhere,
        input_output_aliases={0: 0},
        compiler_params=pltpu.CompilerParams(vmem_limit_bytes=MIB),
        cost_estimate=cost(0.1),
        name="gate",
    )(x, *after)


def inside_mask(latent, exponent):
    quant_step = jnp.exp2(exponent.astype(jnp.float32))
    levels = jnp.floor(latent.astype(jnp.float32) / quant_step + 0.5)
    return (jnp.abs(levels) <= 127.0).astype(jnp.float32)


def shifted(x, axis, size, by):
    return lax.ppermute(x, axis, [(at, (at + by) % size) for at in range(size)])


def load_kernel(streams, spot_ref, *refs):
    outs = refs[3 * streams :]
    for at, out_ref in enumerate(outs):
        parts = refs[3 * at : 3 * at + 3]
        total = parts[0][...].astype(jnp.float32) + parts[1][...].astype(jnp.float32)
        if len(parts[2].shape) == 2:
            total = total + parts[2][...].astype(jnp.float32)
        out_ref[...] = total.astype(NARROW)


def loads(place, aheads, keep, got, moving):
    streams = len(moving)
    width = keep.shape[1]

    def local_spec(at):
        return pl.BlockSpec((PIECE, width), lambda i, spot: (spot[RING_AT + aheads[at] % RINGS], 0))

    whole = pl.BlockSpec((PIECE, width), lambda i, spot: (0, 0))
    in_specs = []
    operands = []
    for at, there in enumerate(moving):
        in_specs += [local_spec(at), local_spec(at)]
        operands += [keep, got]
        if there is None:
            in_specs.append(pl.BlockSpec(memory_space=pltpu.SMEM))
            operands.append(place)
        else:
            in_specs.append(whole)
            operands.append(there)
    shape = jax.ShapeDtypeStruct((PIECE, width), NARROW)
    return pl.pallas_call(
        functools.partial(load_kernel, streams),
        out_shape=(shape,) * streams,
        grid_spec=pltpu.PrefetchScalarGridSpec(
            num_scalar_prefetch=1, grid=(1,), in_specs=in_specs, out_specs=(whole,) * streams
        ),
        compiler_params=pltpu.CompilerParams(vmem_limit_bytes=6 * MIB),
        cost_estimate=cost(2),
        name="loads",
    )(place, *operands)


def settle_kernel(spot_ref, one_ref, two_ref, *refs):
    total = refs[-1]
    total[...] = one_ref[...].astype(jnp.float32) + two_ref[...].astype(jnp.float32)
    line = spot_ref[LINE_AT]
    for at, start in enumerate((line, 1 - line)):
        rows = total[pl.ds(pl.multiple_of(start * ROWS, 8), ROWS), :]
        for block in range(2):
            refs[2 * at + block][...] = rows[:, block * WIDTH : (block + 1) * WIDTH].astype(NARROW)


def settle(place, one, two):
    width = one.shape[1]
    whole = pl.BlockSpec((PIECE, width), lambda i, spot: (0, 0))
    out = pl.BlockSpec((ROWS, WIDTH), lambda i, spot: (0, 0))
    shape = jax.ShapeDtypeStruct((ROWS, WIDTH), NARROW)
    return pl.pallas_call(
        settle_kernel,
        out_shape=(shape,) * 4,
        grid_spec=pltpu.PrefetchScalarGridSpec(
            num_scalar_prefetch=1,
            grid=(1,),
            in_specs=[whole, whole],
            out_specs=(out,) * 4,
            scratch_shapes=[pltpu.VMEM((PIECE, width), jnp.float32)],
        ),
        compiler_params=pltpu.CompilerParams(vmem_limit_bytes=6 * MIB),
        cost_estimate=cost(2),
        name="settle",
    )(place, one, two)


CHUNKS = ((1, 3), (2, 0))


def on_device(
    activations,
    w_query,
    key_weight_latent,
    query_exponent,
    key_column_exponent,
    queries,
    keys,
    teacher_attention_logits,
    document_length,
):
    ring = lax.axis_index("z")
    place = [lax.axis_index(axis) for axis in ("y", "xh", "core", "xl")]
    place = jnp.stack(place + [lax.rem(ring + ahead, RINGS) for ahead in range(RINGS)]).astype(jnp.int32)
    cut = turn(place, activations)
    held = [cut[0]] + [shifted(cut[ahead], "y", 4, ahead) for ahead in PIECE_ORDER[1:]]
    swapped = [shifted(cut[0], "xh", 2, 1)]
    own = head_grads(queries, keys, teacher_attention_logits, document_length, [cut[0]])
    own = gate(own, held[1:] + swapped)
    swapped += [shifted(piece, "xh", 2, 1) for piece in held[1:]]
    pieces = held + swapped
    back = shifted(own, "y", 4, 1)
    fore = shifted(own, "y", 4, 3)
    half = WIDTH // 2
    factors = [
        [own],
        [back],
        [shifted(back[:half], "y", 4, 1), shifted(fore[half:], "y", 4, 3)],
        [fore],
    ]

    mask = inside_mask(w_query, query_exponent[None, :])
    key_mask = inside_mask(key_weight_latent, key_column_exponent[None, :])

    held_terms = []
    after = fore
    wholes = []
    for at, chunk in enumerate(CHUNKS):
        parts = []
        for behind in chunk:
            parts += factors[behind]
        made = []
        for other in (1, 0):
            if at == 0:
                after, whole = first_terms(place, other, pieces, parts, after)
                wholes.append(whole)
            else:
                after = next_terms(wholes[1 - other], parts, after)
            made.append(after)
        held_terms.append((made[1], shifted(made[0], "core", 2, 1)))

    moving = [[None, None], [None, None]]
    for slot in range(4):
        for at, (keep, got) in enumerate(held_terms):
            way = 1 - 2 * at
            aheads = [(4 - slot) * way, (slot - 3) * way]
            long_load, short_load = loads(place, aheads, keep, got, moving[at])
            moving[at] = [
                shifted(long_load, "z", RINGS, way),
                short_load if slot == 3 else shifted(short_load, "z", RINGS, -way),
            ]
    blocks = {}
    for at in range(2):
        made = settle(place, *moving[at])
        for behind, mine, other in zip(CHUNKS[at], made[:2], made[2:]):
            across = [(x * 4 + y, (1 - x) * 4 + (y - behind) % 4) for x in range(2) for y in range(4)]
            other = lax.ppermute(other, ("xl", "y"), across)
            blocks[behind] = (mine if behind == 0 else shifted(mine, "y", 4, 4 - behind), other)
    return finish(place, mask, key_mask, [block for behind in range(4) for block in blocks[behind]])


def solution(mesh):
    fine = jax.sharding.Mesh(mesh.devices.reshape(2, 8, 2, 4, 2), ("xl", "z", "core", "y", "xh"))
    dp = ("xl", "z", "core")
    tensor = ("y", "xh")
    in_specs = (
        P(dp, tensor, None),
        P(dp, tensor),
        P(dp, tensor),
        P(tensor),
        P(tensor),
        P(dp, None, tensor),
        P(dp, None, tensor),
        P(dp, tensor, None, None),
        P(dp, None),
    )
    out_specs = (P(dp, tensor), P(dp, tensor))
    return jax.shard_map(on_device, mesh=fine, in_specs=in_specs, out_specs=out_specs, check_vma=False)
```

```python
import functools
import math

import jax
import jax.numpy as jnp
from jax import lax
from jax.experimental import pallas as pl
from jax.experimental.pallas import tpu as pltpu
from jax.sharding import PartitionSpec as P

SOFT_CAP = 30.0
LOSS_SCALE = 64.0
GROUPS = 2
TOKENS = 512
HEADS = 6
DIM = 96
WIDTH = 672
ROWS = 72
RINGS = 8
BAND = 128
SHARDS = 8
SHARE = 64
NARROW = jnp.bfloat16
MIB = 1024 * 1024
PIECE = 2 * ROWS
LINE_AT = 3
PIECE_ORDER = (0, 1, 3, 2)
RING_AT = 4


def cost(time):
    return pl.CostEstimate(flops=1000, bytes_accessed=int(time * 3.5e6), transcendentals=0)


def spread_tokens(first, second):
    parts = []
    for shard in range(SHARDS):
        parts.append(first[:, shard * SHARE : (shard + 1) * SHARE])
        parts.append(second[:, shard * SHARE : (shard + 1) * SHARE])
    return jnp.concatenate(parts, axis=1).astype(NARROW)


def head_kernel(length_ref, query_ref, key_ref, teacher_ref, *refs):
    out_ref, grad_ref, query_acc, key_acc = refs[-4:]
    head = pl.program_id(0)
    group = pl.program_id(1)

    @pl.when((head == 0) & (group == 0))
    def _():
        grad_ref[...] = jnp.zeros_like(grad_ref)

    ends = [length_ref[group, 0]]
    for document in range(1, length_ref.shape[1]):
        ends.append(ends[-1] + length_ref[group, document])
    query_t = query_ref[0]
    key_t = key_ref[0]
    for first in range(0, TOKENS, BAND):
        low = max(0, first - 2 * BAND)
        high = first + BAND
        token = lax.broadcasted_iota(jnp.int32, (BAND, 1), 0) + first
        start = jnp.zeros_like(token)
        for end in ends:
            start = jnp.where(token >= end, end, start)
        column = lax.broadcasted_iota(jnp.int32, (BAND, high - low), 1) + low
        allowed = (column >= start) & (column <= token)
        dots = lax.dot_general(
            query_t[:, first : first + BAND],
            key_t[:, low:high],
            (((0,), (0,)), ((), ())),
            preferred_element_type=jnp.float32,
        )
        bent = jnp.tanh(dots * (1.0 / (math.sqrt(DIM) * SOFT_CAP)))
        student = jnp.where(allowed, jnp.exp(bent * SOFT_CAP), 0.0)
        logits = teacher_ref[0, 0, first : first + BAND, low:high].astype(jnp.float32)
        teacher = jnp.where(allowed, jnp.exp(logits), 0.0)
        student_scale = 1.0 / jnp.sum(student, axis=1, keepdims=True)
        teacher_scale = 1.0 / jnp.sum(teacher, axis=1, keepdims=True)
        scale = LOSS_SCALE / math.sqrt(DIM)
        slope = scale - scale * (bent * bent)
        grad = (student * student_scale - teacher * teacher_scale) * slope
        grad_ref[first : first + BAND, low:high] = grad.astype(NARROW)
    score_grad = grad_ref[...]
    query_grad = lax.dot_general(
        key_t, score_grad, (((1,), (1,)), ((), ())), preferred_element_type=jnp.float32
    )
    key_grad = lax.dot_general(
        query_t, score_grad, (((1,), (0,)), ((), ())), preferred_element_type=jnp.float32
    )

    @pl.when(head == 0)
    def _():
        key_acc[group] = key_grad

    @pl.when(head != 0)
    def _():
        key_acc[group] = key_acc[group] + key_grad

    @pl.when(group == 0)
    def _():
        query_acc[...] = query_grad

    @pl.when(group == GROUPS - 1)
    def _():
        out_ref[head] = spread_tokens(query_acc[...], query_grad)

    @pl.when((head == HEADS - 1) & (group == GROUPS - 1))
    def _():
        out_ref[HEADS] = spread_tokens(key_acc[0], key_acc[1])


def head_grads(queries, keys, teacher, lengths, after):
    query_t = jnp.swapaxes(queries, 1, 2)
    key_t = jnp.swapaxes(keys, 1, 2)
    shape = (HEADS + 1, DIM, GROUPS * TOKENS)
    out = pl.pallas_call(
        head_kernel,
        out_shape=jax.ShapeDtypeStruct(shape, NARROW),
        grid=(HEADS, GROUPS),
        in_specs=[
            pl.BlockSpec(memory_space=pltpu.SMEM),
            pl.BlockSpec((1, DIM, TOKENS), lambda h, g: (g, h, 0)),
            pl.BlockSpec((1, DIM, TOKENS), lambda h, g: (g, 0, 0)),
            pl.BlockSpec((1, 1, TOKENS, TOKENS), lambda h, g: (g, h, 0, 0)),
        ]
        + [pl.BlockSpec(memory_space=pl.ANY)] * len(after),
        out_specs=pl.BlockSpec(shape, lambda h, g: (0, 0, 0)),
        scratch_shapes=[
            pltpu.VMEM((TOKENS, TOKENS), NARROW),
            pltpu.VMEM((DIM, TOKENS), jnp.float32),
            pltpu.VMEM((GROUPS, DIM, TOKENS), jnp.float32),
        ],
        compiler_params=pltpu.CompilerParams(vmem_limit_bytes=12 * MIB),
        cost_estimate=cost(14),
        name="head_grads",
    )(lengths, query_t, key_t, teacher, *after)
    return out.reshape(WIDTH, GROUPS * TOKENS)


def turn_kernel(place_ref, near_ref, far_ref, *refs):
    turned = refs[4]
    mine = place_ref[0]
    core = place_ref[2]
    lanes = near_ref.shape[2]
    for line, act_ref in enumerate((near_ref, far_ref)):
        block = act_ref[...].reshape(GROUPS * SHARE, lanes).astype(jnp.float32)
        turned[line * lanes : (line + 1) * lanes, :] = block.T
    for ahead in range(4):
        owner = lax.rem(mine + ahead, 4)
        for other in range(2):
            target = core + other - 2 * core * other
            for ring in range(2):
                halves = []
                for line in range(2):
                    start = line * lanes + (ring * 2 + target) * 4 * ROWS + owner * ROWS
                    halves.append(turned[pl.ds(pl.multiple_of(start, 8), ROWS), :])
                refs[ahead][other, ring * PIECE : (ring + 1) * PIECE, :] = jnp.concatenate(halves, axis=0).astype(NARROW)


def turn(place, activations):
    tokens = GROUPS * SHARE
    lanes = 16 * ROWS
    shape = jax.ShapeDtypeStruct((2, RINGS * PIECE, tokens), NARROW)
    return pl.pallas_call(
        turn_kernel,
        out_shape=(shape,) * 4,
        grid=(RINGS // 2,),
        in_specs=[
            pl.BlockSpec(memory_space=pltpu.SMEM),
            pl.BlockSpec((GROUPS, SHARE, lanes), lambda i: (0, 0, i)),
            pl.BlockSpec((GROUPS, SHARE, lanes), lambda i: (0, 0, i + RINGS // 2)),
        ],
        out_specs=(pl.BlockSpec((2, 2 * PIECE, tokens), lambda i: (0, i, 0)),) * 4,
        scratch_shapes=[pltpu.VMEM((2 * lanes, tokens), jnp.float32)],
        compiler_params=pltpu.CompilerParams(vmem_limit_bytes=6 * MIB),
        cost_estimate=cost(3),
        name="turn",
    )(place, *[pltpu.with_memory_space_constraint(activations, pltpu.HBM)] * 2)


def far_off(x):
    return pltpu.with_memory_space_constraint(x, pltpu.HBM)


def join_factors(factors, joined):
    @pl.when(pl.program_id(0) == 0)
    def _():
        row = 0
        for factor in factors:
            joined[row : row + factor.shape[0], :] = factor[...]
            row += factor.shape[0]
        if row < joined.shape[0]:
            joined[row:, :] = jnp.zeros((joined.shape[0] - row, joined.shape[1]), NARROW)


def multiply(rows, joined):
    return lax.dot_general(
        rows, joined[...], (((1,), (1,)), ((), ())), preferred_element_type=jnp.float32
    ).astype(NARROW)


def first_kernel(count, place_ref, *refs):
    pieces = refs[:8]
    out_ref, whole_ref, joined = refs[9 + count :]
    join_factors(refs[8 : 8 + count], joined)
    for at, behind in enumerate(PIECE_ORDER):
        for across in range(2):
            source = lax.rem(place_ref[0] + 4 - behind, 4) * 2 + lax.rem(place_ref[1] + across, 2)
            lane = pl.multiple_of(source * 128, 128)
            whole_ref[:, pl.ds(lane, 128)] = pieces[at + 4 * across][0]
    out_ref[...] = multiply(whole_ref[...], joined)


def next_kernel(count, whole_ref, *refs):
    out_ref, joined = refs[1 + count :]
    join_factors(refs[:count], joined)
    out_ref[...] = multiply(whole_ref[...], joined)


TERM_ROWS = 384


def term_call(kernel, count, rows, width, out_shape, out_specs, in_specs, operands):
    return pl.pallas_call(
        functools.partial(kernel, count),
        out_shape=out_shape,
        grid=(rows // TERM_ROWS,),
        in_specs=in_specs,
        out_specs=out_specs,
        scratch_shapes=[pltpu.VMEM((width, GROUPS * TOKENS), NARROW)],
        compiler_params=pltpu.CompilerParams(vmem_limit_bytes=18 * MIB),
        cost_estimate=cost(6),
        name="terms",
    )(*operands)


def factor_specs(factors):
    return [pl.BlockSpec(factor.shape, lambda i: (0, 0)) for factor in factors] + [pl.BlockSpec(memory_space=pl.ANY)]


def padded_width(factors):
    return -(-sum(factor.shape[0] for factor in factors) // 128) * 128


def first_terms(place, other, pieces, factors, after):
    tokens = GROUPS * TOKENS
    rows = RINGS * PIECE
    width = padded_width(factors)
    return term_call(
        first_kernel,
        len(factors),
        rows,
        width,
        (jax.ShapeDtypeStruct((rows, width), NARROW), jax.ShapeDtypeStruct((rows, tokens), NARROW)),
        (pl.BlockSpec((TERM_ROWS, width), lambda i: (i, 0)), pl.BlockSpec((TERM_ROWS, tokens), lambda i: (i, 0))),
        [pl.BlockSpec(memory_space=pltpu.SMEM)]
        + [pl.BlockSpec((1, TERM_ROWS, GROUPS * SHARE), lambda i: (other, i, 0))] * 8
        + factor_specs(factors),
        (place, *pieces, *factors, after),
    )


def next_terms(whole, factors, after):
    rows, tokens = whole.shape
    width = padded_width(factors)
    return term_call(
        next_kernel,
        len(factors),
        rows,
        width,
        jax.ShapeDtypeStruct((rows, width), NARROW),
        pl.BlockSpec((TERM_ROWS, width), lambda i: (i, 0)),
        [pl.BlockSpec((TERM_ROWS, tokens), lambda i: (i, 0))] + factor_specs(factors),
        (whole, *factors, after),
    )


def finish_kernel(place_ref, mask_ref, key_mask_ref, *refs):
    blocks = refs[:8]
    out_ref, key_out_ref = refs[8:]
    query_width = out_ref.shape[1]
    for behind in range(4):
        owner = lax.rem(place_ref[0] + behind, 4)
        rows = pl.ds(pl.multiple_of(owner * ROWS, 8), ROWS)
        total = blocks[2 * behind][...].astype(jnp.float32) + blocks[2 * behind + 1][...].astype(jnp.float32)
        total = total * (1.0 / LOSS_SCALE)
        out_ref[rows, :] = total[:, :query_width] * mask_ref[rows, :]
        key_out_ref[rows, :] = total[:, query_width:] * key_mask_ref[rows, :]


def finish(place, mask, key_mask, blocks):
    vmem = pl.BlockSpec(memory_space=pltpu.VMEM)
    return pl.pallas_call(
        finish_kernel,
        out_shape=(
            jax.ShapeDtypeStruct(mask.shape, jnp.float32),
            jax.ShapeDtypeStruct(key_mask.shape, jnp.float32),
        ),
        in_specs=[pl.BlockSpec(memory_space=pltpu.SMEM)] + [vmem] * 10,
        out_specs=(vmem, vmem),
        compiler_params=pltpu.CompilerParams(vmem_limit_bytes=6 * MIB),
        cost_estimate=cost(2),
        name="finish",
    )(place, mask, key_mask, *blocks)


def gate_kernel(x_ref, *refs):
    pass


def gate(x, after):
    anywhere = pl.BlockSpec(memory_space=pl.ANY)
    return pl.pallas_call(
        gate_kernel,
        out_shape=jax.ShapeDtypeStruct(x.shape, x.dtype),
        in_specs=[anywhere] * (1 + len(after)),
        out_specs=anywhere,
        input_output_aliases={0: 0},
        compiler_params=pltpu.CompilerParams(vmem_limit_bytes=MIB),
        cost_estimate=cost(0.1),
        name="gate",
    )(x, *after)


def inside_mask(latent, exponent):
    quant_step = jnp.exp2(exponent.astype(jnp.float32))
    levels = jnp.floor(latent.astype(jnp.float32) / quant_step + 0.5)
    return (jnp.abs(levels) <= 127.0).astype(jnp.float32)


def shifted(x, axis, size, by):
    return lax.ppermute(x, axis, [(at, (at + by) % size) for at in range(size)])


def load_kernel(streams, spot_ref, *refs):
    outs = refs[3 * streams :]
    for at, out_ref in enumerate(outs):
        parts = refs[3 * at : 3 * at + 3]
        total = parts[0][...].astype(jnp.float32) + parts[1][...].astype(jnp.float32)
        if len(parts[2].shape) == 2:
            total = total + parts[2][...].astype(jnp.float32)
        out_ref[...] = total.astype(NARROW)


def loads(place, aheads, keep, got, moving):
    streams = len(moving)
    width = keep.shape[1]

    def local_spec(at):
        return pl.BlockSpec((PIECE, width), lambda i, spot: (spot[RING_AT + aheads[at] % RINGS], 0))

    whole = pl.BlockSpec((PIECE, width), lambda i, spot: (0, 0))
    in_specs = []
    operands = []
    for at, there in enumerate(moving):
        in_specs += [local_spec(at), local_spec(at)]
        operands += [keep, got]
        if there is None:
            in_specs.append(pl.BlockSpec(memory_space=pltpu.SMEM))
            operands.append(place)
        else:
            in_specs.append(whole)
            operands.append(there)
    shape = jax.ShapeDtypeStruct((PIECE, width), NARROW)
    return pl.pallas_call(
        functools.partial(load_kernel, streams),
        out_shape=(shape,) * streams,
        grid_spec=pltpu.PrefetchScalarGridSpec(
            num_scalar_prefetch=1, grid=(1,), in_specs=in_specs, out_specs=(whole,) * streams
        ),
        compiler_params=pltpu.CompilerParams(vmem_limit_bytes=6 * MIB),
        cost_estimate=cost(2),
        name="loads",
    )(place, *operands)


def settle_kernel(spot_ref, keep_ref, got_ref, one_ref, two_ref, *refs):
    total = refs[-1]
    total[...] = (
        keep_ref[...].astype(jnp.float32)
        + got_ref[...].astype(jnp.float32)
        + one_ref[...].astype(jnp.float32)
        + two_ref[...].astype(jnp.float32)
    )
    line = spot_ref[LINE_AT]
    for at, start in enumerate((line, 1 - line)):
        rows = total[pl.ds(pl.multiple_of(start * ROWS, 8), ROWS), :]
        for block in range(2):
            refs[2 * at + block][...] = rows[:, block * WIDTH : (block + 1) * WIDTH].astype(NARROW)


def settle(place, keep, got, one, two):
    width = keep.shape[1]
    local = pl.BlockSpec((PIECE, width), lambda i, spot: (spot[RING_AT], 0))
    whole = pl.BlockSpec((PIECE, width), lambda i, spot: (0, 0))
    out = pl.BlockSpec((ROWS, WIDTH), lambda i, spot: (0, 0))
    shape = jax.ShapeDtypeStruct((ROWS, WIDTH), NARROW)
    return pl.pallas_call(
        settle_kernel,
        out_shape=(shape,) * 4,
        grid_spec=pltpu.PrefetchScalarGridSpec(
            num_scalar_prefetch=1,
            grid=(1,),
            in_specs=[local, local, whole, whole],
            out_specs=(out,) * 4,
            scratch_shapes=[pltpu.VMEM((PIECE, width), jnp.float32)],
        ),
        compiler_params=pltpu.CompilerParams(vmem_limit_bytes=6 * MIB),
        cost_estimate=cost(2),
        name="settle",
    )(place, keep, got, one, two)


CHUNKS = ((1, 3), (2, 0))


def on_device(
    activations,
    w_query,
    key_weight_latent,
    query_exponent,
    key_column_exponent,
    queries,
    keys,
    teacher_attention_logits,
    document_length,
):
    ring = lax.axis_index("z")
    place = [lax.axis_index(axis) for axis in ("y", "xh", "core", "xl")]
    place = jnp.stack(place + [lax.rem(ring + ahead, RINGS) for ahead in range(RINGS)]).astype(jnp.int32)
    cut = turn(place, activations)
    held = [cut[0]] + [shifted(cut[ahead], "y", 4, ahead) for ahead in PIECE_ORDER[1:]]
    swapped = [shifted(cut[0], "xh", 2, 1)]
    own = head_grads(queries, keys, teacher_attention_logits, document_length, [cut[0]])
    own = gate(own, held[1:] + swapped)
    swapped += [shifted(piece, "xh", 2, 1) for piece in held[1:]]
    pieces = held + swapped
    back = shifted(own, "y", 4, 1)
    fore = shifted(own, "y", 4, 3)
    half = WIDTH // 2
    factors = [
        [own],
        [back],
        [shifted(back[:half], "y", 4, 1), shifted(fore[half:], "y", 4, 3)],
        [fore],
    ]

    mask = inside_mask(w_query, query_exponent[None, :])
    key_mask = inside_mask(key_weight_latent, key_column_exponent[None, :])

    held_terms = []
    after = fore
    wholes = []
    for at, chunk in enumerate(CHUNKS):
        parts = []
        for behind in chunk:
            parts += factors[behind]
        made = []
        for other in (1, 0):
            if at == 0:
                after, whole = first_terms(place, other, pieces, parts, after)
                wholes.append(whole)
            else:
                after = next_terms(wholes[1 - other], parts, after)
            made.append(after)
        held_terms.append((made[1], shifted(made[0], "core", 2, 1)))

    moving = [[None, None], [None, None]]
    for slot in range(4):
        for at, (keep, got) in enumerate(held_terms):
            way = 1 - 2 * at
            aheads = [(4 - slot) * way, (slot - 3) * way]
            count = 2 if slot < 3 else 1
            sums = loads(place, aheads[:count], keep, got, moving[at][:count])
            for stream, load in enumerate(sums):
                moving[at][stream] = shifted(load, "z", RINGS, -way if stream else way)
    blocks = {}
    for at, (keep, got) in enumerate(held_terms):
        made = settle(place, keep, got, *moving[at])
        for behind, mine, other in zip(CHUNKS[at], made[:2], made[2:]):
            across = [(x * 4 + y, (1 - x) * 4 + (y - behind) % 4) for x in range(2) for y in range(4)]
            other = lax.ppermute(other, ("xl", "y"), across)
            blocks[behind] = (mine if behind == 0 else shifted(mine, "y", 4, 4 - behind), other)
    return finish(place, mask, key_mask, [block for behind in range(4) for block in blocks[behind]])


def solution(mesh):
    fine = jax.sharding.Mesh(mesh.devices.reshape(2, 8, 2, 4, 2), ("xl", "z", "core", "y", "xh"))
    dp = ("xl", "z", "core")
    tensor = ("y", "xh")
    in_specs = (
        P(dp, tensor, None),
        P(dp, tensor),
        P(dp, tensor),
        P(tensor),
        P(tensor),
        P(dp, None, tensor),
        P(dp, None, tensor),
        P(dp, tensor, None, None),
        P(dp, None),
    )
    out_specs = (P(dp, tensor), P(dp, tensor))
    return jax.shard_map(on_device, mesh=fine, in_specs=in_specs, out_specs=out_specs, check_vma=False)
```

```python
import functools
import math

import jax
import jax.numpy as jnp
from jax import lax
from jax.experimental import pallas as pl
from jax.experimental.pallas import tpu as pltpu
from jax.sharding import PartitionSpec as P

SOFT_CAP = 30.0
LOSS_SCALE = 64.0
GROUPS = 2
TOKENS = 512
HEADS = 6
DIM = 96
WIDTH = 672
ROWS = 72
RINGS = 8
BAND = 128
SHARDS = 8
SHARE = 64
NARROW = jnp.bfloat16
MIB = 1024 * 1024
PIECE = 2 * ROWS
LINE_AT = 3
PIECE_ORDER = (0, 1, 3, 2)
RING_AT = 4


def cost(time):
    return pl.CostEstimate(flops=1000, bytes_accessed=int(time * 3.5e6), transcendentals=0)


def spread_tokens(first, second):
    parts = []
    for shard in range(SHARDS):
        parts.append(first[:, shard * SHARE : (shard + 1) * SHARE])
        parts.append(second[:, shard * SHARE : (shard + 1) * SHARE])
    return jnp.concatenate(parts, axis=1).astype(NARROW)


def head_kernel(length_ref, query_ref, key_ref, teacher_ref, *refs):
    out_ref, grad_ref, query_acc, key_acc = refs[-4:]
    head = pl.program_id(0)
    group = pl.program_id(1)

    @pl.when((head == 0) & (group == 0))
    def _():
        grad_ref[...] = jnp.zeros_like(grad_ref)

    ends = [length_ref[group, 0]]
    for document in range(1, length_ref.shape[1]):
        ends.append(ends[-1] + length_ref[group, document])
    query_t = query_ref[0]
    key_t = key_ref[0]
    for first in range(0, TOKENS, BAND):
        low = max(0, first - 2 * BAND)
        high = first + BAND
        token = lax.broadcasted_iota(jnp.int32, (BAND, 1), 0) + first
        start = jnp.zeros_like(token)
        for end in ends:
            start = jnp.where(token >= end, end, start)
        column = lax.broadcasted_iota(jnp.int32, (BAND, high - low), 1) + low
        allowed = (column >= start) & (column <= token)
        dots = lax.dot_general(
            query_t[:, first : first + BAND],
            key_t[:, low:high],
            (((0,), (0,)), ((), ())),
            preferred_element_type=jnp.float32,
        )
        bent = jnp.tanh(dots * (1.0 / (math.sqrt(DIM) * SOFT_CAP)))
        student = jnp.where(allowed, jnp.exp(bent * SOFT_CAP), 0.0)
        logits = teacher_ref[0, 0, first : first + BAND, low:high].astype(jnp.float32)
        teacher = jnp.where(allowed, jnp.exp(logits), 0.0)
        student_scale = 1.0 / jnp.sum(student, axis=1, keepdims=True)
        teacher_scale = 1.0 / jnp.sum(teacher, axis=1, keepdims=True)
        scale = LOSS_SCALE / math.sqrt(DIM)
        slope = scale - scale * (bent * bent)
        grad = (student * student_scale - teacher * teacher_scale) * slope
        grad_ref[first : first + BAND, low:high] = grad.astype(NARROW)
    score_grad = grad_ref[...]
    query_grad = lax.dot_general(
        key_t, score_grad, (((1,), (1,)), ((), ())), preferred_element_type=jnp.float32
    )
    key_grad = lax.dot_general(
        query_t, score_grad, (((1,), (0,)), ((), ())), preferred_element_type=jnp.float32
    )

    @pl.when(head == 0)
    def _():
        key_acc[group] = key_grad

    @pl.when(head != 0)
    def _():
        key_acc[group] = key_acc[group] + key_grad

    @pl.when(group == 0)
    def _():
        query_acc[...] = query_grad

    @pl.when(group == GROUPS - 1)
    def _():
        out_ref[head] = spread_tokens(query_acc[...], query_grad)

    @pl.when((head == HEADS - 1) & (group == GROUPS - 1))
    def _():
        out_ref[HEADS] = spread_tokens(key_acc[0], key_acc[1])


def head_grads(queries, keys, teacher, lengths, after):
    query_t = jnp.swapaxes(queries, 1, 2)
    key_t = jnp.swapaxes(keys, 1, 2)
    shape = (HEADS + 1, DIM, GROUPS * TOKENS)
    out = pl.pallas_call(
        head_kernel,
        out_shape=jax.ShapeDtypeStruct(shape, NARROW),
        grid=(HEADS, GROUPS),
        in_specs=[
            pl.BlockSpec(memory_space=pltpu.SMEM),
            pl.BlockSpec((1, DIM, TOKENS), lambda h, g: (g, h, 0)),
            pl.BlockSpec((1, DIM, TOKENS), lambda h, g: (g, 0, 0)),
            pl.BlockSpec((1, 1, TOKENS, TOKENS), lambda h, g: (g, h, 0, 0)),
        ]
        + [pl.BlockSpec(memory_space=pl.ANY)] * len(after),
        out_specs=pl.BlockSpec(shape, lambda h, g: (0, 0, 0)),
        scratch_shapes=[
            pltpu.VMEM((TOKENS, TOKENS), NARROW),
            pltpu.VMEM((DIM, TOKENS), jnp.float32),
            pltpu.VMEM((GROUPS, DIM, TOKENS), jnp.float32),
        ],
        compiler_params=pltpu.CompilerParams(vmem_limit_bytes=12 * MIB),
        cost_estimate=cost(14),
        name="head_grads",
    )(lengths, query_t, key_t, teacher, *after)
    return out.reshape(WIDTH, GROUPS * TOKENS)


def turn_kernel(place_ref, near_ref, far_ref, *refs):
    turned = refs[4]
    mine = place_ref[0]
    core = place_ref[2]
    lanes = near_ref.shape[2]
    for line, act_ref in enumerate((near_ref, far_ref)):
        block = act_ref[...].reshape(GROUPS * SHARE, lanes).astype(jnp.float32)
        turned[line * lanes : (line + 1) * lanes, :] = block.T
    for ahead in range(4):
        owner = lax.rem(mine + ahead, 4)
        for other in range(2):
            target = core + other - 2 * core * other
            for ring in range(2):
                halves = []
                for line in range(2):
                    start = line * lanes + (ring * 2 + target) * 4 * ROWS + owner * ROWS
                    halves.append(turned[pl.ds(pl.multiple_of(start, 8), ROWS), :])
                refs[ahead][other, ring * PIECE : (ring + 1) * PIECE, :] = jnp.concatenate(halves, axis=0).astype(NARROW)


def turn(place, activations):
    tokens = GROUPS * SHARE
    lanes = 16 * ROWS
    shape = jax.ShapeDtypeStruct((2, RINGS * PIECE, tokens), NARROW)
    return pl.pallas_call(
        turn_kernel,
        out_shape=(shape,) * 4,
        grid=(RINGS // 2,),
        in_specs=[
            pl.BlockSpec(memory_space=pltpu.SMEM),
            pl.BlockSpec((GROUPS, SHARE, lanes), lambda i: (0, 0, i)),
            pl.BlockSpec((GROUPS, SHARE, lanes), lambda i: (0, 0, i + RINGS // 2)),
        ],
        out_specs=(pl.BlockSpec((2, 2 * PIECE, tokens), lambda i: (0, i, 0)),) * 4,
        scratch_shapes=[pltpu.VMEM((2 * lanes, tokens), jnp.float32)],
        compiler_params=pltpu.CompilerParams(vmem_limit_bytes=6 * MIB),
        cost_estimate=cost(3),
        name="turn",
    )(place, *[pltpu.with_memory_space_constraint(activations, pltpu.HBM)] * 2)


def far_off(x):
    return pltpu.with_memory_space_constraint(x, pltpu.HBM)


def join_factors(factors, joined):
    @pl.when(pl.program_id(0) == 0)
    def _():
        row = 0
        for factor in factors:
            joined[row : row + factor.shape[0], :] = factor[...]
            row += factor.shape[0]
        if row < joined.shape[0]:
            joined[row:, :] = jnp.zeros((joined.shape[0] - row, joined.shape[1]), NARROW)


def multiply(rows, joined):
    return lax.dot_general(
        rows, joined[...], (((1,), (1,)), ((), ())), preferred_element_type=jnp.float32
    ).astype(NARROW)


def first_kernel(count, place_ref, *refs):
    pieces = refs[:8]
    out_ref, whole_ref, joined = refs[9 + count :]
    join_factors(refs[8 : 8 + count], joined)
    for at, behind in enumerate(PIECE_ORDER):
        for across in range(2):
            source = lax.rem(place_ref[0] + 4 - behind, 4) * 2 + lax.rem(place_ref[1] + across, 2)
            lane = pl.multiple_of(source * 128, 128)
            whole_ref[:, pl.ds(lane, 128)] = pieces[at + 4 * across][0]
    out_ref[...] = multiply(whole_ref[...], joined)


def next_kernel(count, whole_ref, *refs):
    out_ref, joined = refs[1 + count :]
    join_factors(refs[:count], joined)
    out_ref[...] = multiply(whole_ref[...], joined)


TERM_ROWS = 384


def term_call(kernel, count, rows, width, out_shape, out_specs, in_specs, operands):
    return pl.pallas_call(
        functools.partial(kernel, count),
        out_shape=out_shape,
        grid=(rows // TERM_ROWS,),
        in_specs=in_specs,
        out_specs=out_specs,
        scratch_shapes=[pltpu.VMEM((width, GROUPS * TOKENS), NARROW)],
        compiler_params=pltpu.CompilerParams(vmem_limit_bytes=18 * MIB),
        cost_estimate=cost(6),
        name="terms",
    )(*operands)


def factor_specs(factors):
    return [pl.BlockSpec(factor.shape, lambda i: (0, 0)) for factor in factors] + [pl.BlockSpec(memory_space=pl.ANY)]


def padded_width(factors):
    return -(-sum(factor.shape[0] for factor in factors) // 128) * 128


def first_terms(place, other, pieces, factors, after):
    tokens = GROUPS * TOKENS
    rows = RINGS * PIECE
    width = padded_width(factors)
    return term_call(
        first_kernel,
        len(factors),
        rows,
        width,
        (jax.ShapeDtypeStruct((rows, width), NARROW), jax.ShapeDtypeStruct((rows, tokens), NARROW)),
        (pl.BlockSpec((TERM_ROWS, width), lambda i: (i, 0)), pl.BlockSpec((TERM_ROWS, tokens), lambda i: (i, 0))),
        [pl.BlockSpec(memory_space=pltpu.SMEM)]
        + [pl.BlockSpec((1, TERM_ROWS, GROUPS * SHARE), lambda i: (other, i, 0))] * 8
        + factor_specs(factors),
        (place, *pieces, *factors, after),
    )


def next_terms(whole, factors, after):
    rows, tokens = whole.shape
    width = padded_width(factors)
    return term_call(
        next_kernel,
        len(factors),
        rows,
        width,
        jax.ShapeDtypeStruct((rows, width), NARROW),
        pl.BlockSpec((TERM_ROWS, width), lambda i: (i, 0)),
        [pl.BlockSpec((TERM_ROWS, tokens), lambda i: (i, 0))] + factor_specs(factors),
        (whole, *factors, after),
    )


def finish_kernel(place_ref, mask_ref, key_mask_ref, *refs):
    blocks = refs[:8]
    out_ref, key_out_ref = refs[8:]
    query_width = out_ref.shape[1]
    for behind in range(4):
        owner = lax.rem(place_ref[0] + behind, 4)
        rows = pl.ds(pl.multiple_of(owner * ROWS, 8), ROWS)
        total = blocks[2 * behind][...].astype(jnp.float32) + blocks[2 * behind + 1][...].astype(jnp.float32)
        total = total * (1.0 / LOSS_SCALE)
        out_ref[rows, :] = total[:, :query_width] * mask_ref[rows, :]
        key_out_ref[rows, :] = total[:, query_width:] * key_mask_ref[rows, :]


def finish(place, mask, key_mask, blocks):
    vmem = pl.BlockSpec(memory_space=pltpu.VMEM)
    return pl.pallas_call(
        finish_kernel,
        out_shape=(
            jax.ShapeDtypeStruct(mask.shape, jnp.float32),
            jax.ShapeDtypeStruct(key_mask.shape, jnp.float32),
        ),
        in_specs=[pl.BlockSpec(memory_space=pltpu.SMEM)] + [vmem] * 10,
        out_specs=(vmem, vmem),
        compiler_params=pltpu.CompilerParams(vmem_limit_bytes=6 * MIB),
        cost_estimate=cost(2),
        name="finish",
    )(place, mask, key_mask, *blocks)


def gate_kernel(x_ref, *refs):
    pass


def gate(x, after):
    anywhere = pl.BlockSpec(memory_space=pl.ANY)
    return pl.pallas_call(
        gate_kernel,
        out_shape=jax.ShapeDtypeStruct(x.shape, x.dtype),
        in_specs=[anywhere] * (1 + len(after)),
        out_specs=anywhere,
        input_output_aliases={0: 0},
        compiler_params=pltpu.CompilerParams(vmem_limit_bytes=MIB),
        cost_estimate=cost(0.1),
        name="gate",
    )(x, *after)


def inside_mask(latent, exponent):
    quant_step = jnp.exp2(exponent.astype(jnp.float32))
    levels = jnp.floor(latent.astype(jnp.float32) / quant_step + 0.5)
    return (jnp.abs(levels) <= 127.0).astype(jnp.float32)


def shifted(x, axis, size, by):
    return lax.ppermute(x, axis, [(at, (at + by) % size) for at in range(size)])


def load_kernel(streams, spot_ref, *refs):
    outs = refs[len(refs) - streams :]
    for at, out_ref in enumerate(outs):
        parts = refs[3 * at : 3 * at + 3]
        total = parts[0][...].astype(jnp.float32) + parts[1][...].astype(jnp.float32)
        if len(parts[2].shape) == 2:
            total = total + parts[2][...].astype(jnp.float32)
        out_ref[...] = total.astype(NARROW)


def loads(place, aheads, keep, got, moving, after=()):
    streams = len(moving)
    width = keep.shape[1]

    def local_spec(at):
        return pl.BlockSpec((PIECE, width), lambda i, spot: (spot[RING_AT + aheads[at] % RINGS], 0))

    whole = pl.BlockSpec((PIECE, width), lambda i, spot: (0, 0))
    in_specs = []
    operands = []
    for at, there in enumerate(moving):
        in_specs += [local_spec(at), local_spec(at)]
        operands += [keep, got]
        if there is None:
            in_specs.append(pl.BlockSpec(memory_space=pltpu.SMEM))
            operands.append(place)
        else:
            in_specs.append(whole)
            operands.append(there)
    for there in after:
        in_specs.append(pl.BlockSpec(memory_space=pl.ANY))
        operands.append(there)
    shape = jax.ShapeDtypeStruct((PIECE, width), NARROW)
    return pl.pallas_call(
        functools.partial(load_kernel, streams),
        out_shape=(shape,) * streams,
        grid_spec=pltpu.PrefetchScalarGridSpec(
            num_scalar_prefetch=1, grid=(1,), in_specs=in_specs, out_specs=(whole,) * streams
        ),
        compiler_params=pltpu.CompilerParams(vmem_limit_bytes=6 * MIB),
        cost_estimate=cost(2),
        name="loads",
    )(place, *operands)


def settle_kernel(spot_ref, keep_ref, got_ref, one_ref, two_ref, *refs):
    total = refs[-1]
    total[...] = (
        keep_ref[...].astype(jnp.float32)
        + got_ref[...].astype(jnp.float32)
        + one_ref[...].astype(jnp.float32)
        + two_ref[...].astype(jnp.float32)
    )
    line = spot_ref[LINE_AT]
    for at, start in enumerate((line, 1 - line)):
        rows = total[pl.ds(pl.multiple_of(start * ROWS, 8), ROWS), :]
        for block in range(2):
            refs[2 * at + block][...] = rows[:, block * WIDTH : (block + 1) * WIDTH].astype(NARROW)


def settle(place, keep, got, one, two):
    width = keep.shape[1]
    local = pl.BlockSpec((PIECE, width), lambda i, spot: (spot[RING_AT], 0))
    whole = pl.BlockSpec((PIECE, width), lambda i, spot: (0, 0))
    out = pl.BlockSpec((ROWS, WIDTH), lambda i, spot: (0, 0))
    shape = jax.ShapeDtypeStruct((ROWS, WIDTH), NARROW)
    return pl.pallas_call(
        settle_kernel,
        out_shape=(shape,) * 4,
        grid_spec=pltpu.PrefetchScalarGridSpec(
            num_scalar_prefetch=1,
            grid=(1,),
            in_specs=[local, local, whole, whole],
            out_specs=(out,) * 4,
            scratch_shapes=[pltpu.VMEM((PIECE, width), jnp.float32)],
        ),
        compiler_params=pltpu.CompilerParams(vmem_limit_bytes=6 * MIB),
        cost_estimate=cost(2),
        name="settle",
    )(place, keep, got, one, two)


CHUNKS = ((1, 3), (2, 0))


def on_device(
    activations,
    w_query,
    key_weight_latent,
    query_exponent,
    key_column_exponent,
    queries,
    keys,
    teacher_attention_logits,
    document_length,
):
    ring = lax.axis_index("z")
    place = [lax.axis_index(axis) for axis in ("y", "xh", "core", "xl")]
    place = jnp.stack(place + [lax.rem(ring + ahead, RINGS) for ahead in range(RINGS)]).astype(jnp.int32)
    cut = turn(place, activations)
    held = [cut[0]] + [shifted(cut[ahead], "y", 4, ahead) for ahead in PIECE_ORDER[1:]]
    swapped = [shifted(cut[0], "xh", 2, 1)]
    own = head_grads(queries, keys, teacher_attention_logits, document_length, [cut[0]])
    own = gate(own, held[1:] + swapped)
    swapped += [shifted(piece, "xh", 2, 1) for piece in held[1:]]
    pieces = held + swapped
    back = shifted(own, "y", 4, 1)
    fore = shifted(own, "y", 4, 3)
    half = WIDTH // 2
    factors = [
        [own],
        [back],
        [shifted(back[:half], "y", 4, 1), shifted(fore[half:], "y", 4, 3)],
        [fore],
    ]

    mask = inside_mask(w_query, query_exponent[None, :])
    key_mask = inside_mask(key_weight_latent, key_column_exponent[None, :])

    held_terms = []
    after = fore
    wholes = []
    for at, chunk in enumerate(CHUNKS):
        parts = []
        for behind in chunk:
            parts += factors[behind]
        made = []
        for other in (1, 0):
            if at == 0:
                after, whole = first_terms(place, other, pieces, parts, after)
                wholes.append(whole)
            else:
                after = next_terms(wholes[1 - other], parts, after)
            made.append(after)
        held_terms.append((made[1], shifted(made[0], "core", 2, 1)))

    moving = [[None, None], [None, None]]
    for slot in range(4):
        for at, (keep, got) in enumerate(held_terms):
            way = 1 - 2 * at
            aheads = [(4 - slot) * way, (slot - 3) * way]
            count = 2 if slot < 3 else 1
            after = moving[0][1:] if slot == 3 and at == 1 else []
            sums = loads(place, aheads[:count], keep, got, moving[at][:count], after)
            for stream, load in enumerate(sums):
                moving[at][stream] = shifted(load, "z", RINGS, -way if stream else way)
    blocks = {}
    for at, (keep, got) in enumerate(held_terms):
        made = settle(place, keep, got, *moving[at])
        for behind, mine, other in zip(CHUNKS[at], made[:2], made[2:]):
            across = [(x * 4 + y, (1 - x) * 4 + (y - behind) % 4) for x in range(2) for y in range(4)]
            other = lax.ppermute(other, ("xl", "y"), across)
            blocks[behind] = (mine if behind == 0 else shifted(mine, "y", 4, 4 - behind), other)
    return finish(place, mask, key_mask, [block for behind in range(4) for block in blocks[behind]])


def solution(mesh):
    fine = jax.sharding.Mesh(mesh.devices.reshape(2, 8, 2, 4, 2), ("xl", "z", "core", "y", "xh"))
    dp = ("xl", "z", "core")
    tensor = ("y", "xh")
    in_specs = (
        P(dp, tensor, None),
        P(dp, tensor),
        P(dp, tensor),
        P(tensor),
        P(tensor),
        P(dp, None, tensor),
        P(dp, None, tensor),
        P(dp, tensor, None, None),
        P(dp, None),
    )
    out_specs = (P(dp, tensor), P(dp, tensor))
    return jax.shard_map(on_device, mesh=fine, in_specs=in_specs, out_specs=out_specs, check_vma=False)
```
